32 devices in a mesh: ctx: 8 (over y, x, core), head: 4 (over z).
Axes of the slice: x: 2, y: 2, z: 4, core: 2. Of those that a mesh axis runs over, the one named last changes fastest.
Arguments:
- queries: bfloat16 [1024, 1024], P(('ctx', 'head')), may hold values from -6 to 6
- keys: bfloat16 [1024, 1024], P(('ctx', 'head')), may hold values from -6 to 6
- values: bfloat16 [1024, 2048], P(('ctx', 'head')), may hold values from -6 to 6
- grad_out: bfloat16 [1024, 2048], P('ctx', 'head'), may hold values from -6 to 6
- log_decay: float32 [4, 1024], P('head', 'ctx'), may hold values from -1 to 0
- doc_lengths: int32 [32], replicated, may hold values from 1 to 256, 1024 in all
Outputs:
- retained: bfloat16 [1024, 2048], P('ctx', 'head')
- query_gradient: bfloat16 [1024, 1024], P('ctx', 'head')
- grad_k: bfloat16 [1024, 1024], P('ctx', 'head')
- value_gradient: bfloat16 [1024, 2048], P('ctx', 'head')
The draws below stay inside these ranges and needn't reach their ends.
Inputs may be any that keep to these rules, and one draw needn't show every extreme that they name: `doc_lengths`: the 32 lengths sum to 1024; the largest is exactly 256.
All inputs are finite; a program needn't handle non-finite values.
Results may differ from the reference program's by a relative error of at most 0.0056.
Values may be sent and summed in bfloat16 or wider, within the bound.
A program may use at most 64 MiB of HBM per device.

```python
import math
import jax
import jax.numpy as jnp
import numpy as np
from jax import lax

DK = 256
DV = 512
BLOCK = 128
NDOCS = 32
TOK_DEV = 128
HEADS = 4
WINDOW_TOKENS = 1024
LONGEST = 256


spike_total_count = 3


def draw_log_decay(key, part):
    key_sequence = jax.random.split(key, 7)
    order = jax.random.permutation(key_sequence[0], HEADS)
    fast_heads = order < max(HEADS // 2, 1)
    fast_rate = jnp.exp(jax.random.uniform(key_sequence[1], (HEADS,), jnp.float32, math.log(1.0 / 50.0), math.log(1.0 / 30.0)))
    slow_rate = jnp.exp(jax.random.uniform(key_sequence[2], (HEADS,), jnp.float32, math.log(0.05), math.log(0.3))) / WINDOW_TOKENS
    baseline_decay_rate = jnp.where(fast_heads, fast_rate, slow_rate)
    shard_count = WINDOW_TOKENS // TOK_DEV
    partition_gain = jnp.exp(jax.random.uniform(key_sequence[3], (HEADS, shard_count), jnp.float32, math.log(0.5), math.log(2.0)))
    partition_gain = jnp.repeat(partition_gain, TOK_DEV, axis=1)
    jitter_amplitude = jnp.exp(jax.random.uniform(key_sequence[4], (HEADS, WINDOW_TOKENS), jnp.float32, math.log(0.6), math.log(1.3)))
    spike_locations = jax.random.randint(key_sequence[5], (spike_total_count,), 0, WINDOW_TOKENS)
    spike_removals = jax.random.uniform(key_sequence[6], (spike_total_count,), jnp.float32, math.log(0.5), math.log(0.8))
    spike_matches = (jnp.arange(WINDOW_TOKENS, dtype=jnp.int32)[:, None] == spike_locations[None, :]).astype(jnp.float32)
    spike_events = jnp.sum(spike_matches * spike_removals[None, :], axis=1)
    return -baseline_decay_rate[:, None] * partition_gain * jitter_amplitude + spike_events[None, :]


def shard_levels(own_key, shape, pieces, low, top_value):
    def one(position, blocks):
        steps = jax.random.uniform(jax.random.fold_in(jax.random.fold_in(own_key, 6), position), (blocks,), jnp.float32, low / len(pieces), top_value / len(pieces))
        return jnp.repeat(jnp.exp(steps), shape[position] // blocks).reshape((-1,) + (1,) * (len(shape) - position - 1))

    gain = one(*pieces[0])
    for cut in pieces[1:]:
        gain = gain * one(*cut)
    return gain


def length_profile(amount, total, most, skew):
    weights = [(1 << 20) // math.isqrt(rank ** skew) + 1 for rank in range(2, amount + 1)]
    surplus, counts = total - most - (amount - 1), [1] * (amount - 1)
    while surplus > 0:
        free = [i for i in range(amount - 1) if counts[i] < most]
        whole, budget = sum([weights[i] for i in free]), surplus
        for i in free:
            extra = min(most - counts[i], max(1, budget * weights[i] // whole), surplus)
            counts[i] = counts[i] + extra
            surplus = surplus - extra
    return np.array([most] + counts)


def uneven_parts(key, number_of, total, most, skew):
    if number_of == 2:
        one = jax.random.randint(key, (), max(1, total - most), min(most, total - 1) + 1)
        return jnp.stack([one, total - one])
    tallies = jnp.asarray(length_profile(number_of, total, most, skew), jnp.int32)
    couples = (number_of - 1) // 2
    source_of, taker = tallies[1:1 + 2 * couples:2], tallies[2:2 + 2 * couples:2]
    room = jnp.minimum(source_of - 1, most - taker)
    shifted = jax.random.randint(jax.random.fold_in(key, 1), (couples,), 0, 1 << 20) % (room + 1)
    tallies = tallies.at[1:1 + 2 * couples:2].set(source_of - shifted).at[2:2 + 2 * couples:2].set(taker + shifted)
    return tallies[jax.random.permutation(jax.random.fold_in(key, 2), number_of)]


def noise(key, shape, deviation, most, cuts=(), kind=jnp.bfloat16):
    drawn = deviation * jax.random.normal(key, shape, jnp.float32)
    if cuts:
        drawn = drawn * shard_levels(key, shape, cuts, -0.22, 0.18)
    return jnp.clip(drawn, -most, most).astype(kind)


def setup_inputs(seed: int = 0) -> dict:
    seeds = jax.random.split(jax.random.key(seed), 7)
    return {
        "queries": noise(seeds[0], (WINDOW_TOKENS, HEADS * DK), 1.0, 6.0, ((0, 32),)),
        "keys": noise(seeds[1], (WINDOW_TOKENS, HEADS * DK), 1.0, 6.0, ((0, 32),)),
        "values": noise(seeds[2], (WINDOW_TOKENS, HEADS * DV), 1.0, 6.0, ((0, 32),)),
        "grad_out": noise(seeds[3], (WINDOW_TOKENS, HEADS * DV), 1.0, 6.0, ((0, 8), (1, 4))),
        "log_decay": draw_log_decay(jax.random.fold_in(seeds[6], 71), 0),
        "doc_lengths": uneven_parts(seeds[5], NDOCS, WINDOW_TOKENS, LONGEST, 2).astype(jnp.int32),
    }


def rounded(values):
    return lax.optimization_barrier(values.astype(jnp.bfloat16)).astype(jnp.float32)


def document_ids(doc_lengths, first_place, span_length):
    starts = jnp.cumsum(doc_lengths, dtype=jnp.int32) - doc_lengths
    places = first_place - 1 + jnp.arange(span_length + 1, dtype=jnp.int32)
    return jnp.sum((starts[None, :] <= places[:, None]).astype(jnp.int32), axis=1) - 1


def decay_tables(log_rates, doc_ids, block_size, score_scaling):
    block_count = log_rates.shape[0] // block_size
    cumulated = jnp.cumsum(log_rates.reshape(block_count, block_size), axis=1)
    before = doc_ids[0:block_count * block_size:block_size]
    own_ids = doc_ids[1:].reshape(block_count, block_size)
    carried = (own_ids == before[:, None]).astype(jnp.float32)
    last_ids = own_ids[:, block_size - 1]
    tail_mask = (own_ids == last_ids[:, None]).astype(jnp.float32)
    block_decay = jnp.exp(cumulated[:, block_size - 1]) * carried[:, block_size - 1]
    row_index = lax.broadcasted_iota(jnp.int32, (block_size, block_size), 0)
    column_index = lax.broadcasted_iota(jnp.int32, (block_size, block_size), 1)
    inside = (own_ids[:, :, None] == own_ids[:, None, :]) & (row_index >= column_index)[None]
    decay_gaps = cumulated[:, :, None] - cumulated[:, None, :]
    weights = jnp.where(inside, jnp.exp(jnp.where(inside, decay_gaps, 0.0)), 0.0) * score_scaling
    per_head_decay_rate = jnp.exp(cumulated) * carried
    tail_decay = jnp.exp(cumulated[:, block_size - 1:] - cumulated) * tail_mask
    return weights, per_head_decay_rate, tail_decay, block_decay


def forward_step(state, inputs):
    decay, update = inputs
    return decay * state + update, state


def reference(queries, keys, values, grad_out, log_decay, doc_lengths):
    doc_ids = document_ids(doc_lengths, 0, WINDOW_TOKENS)
    block_count = WINDOW_TOKENS // BLOCK
    score_scaling = (DK * BLOCK) ** -0.5

    def one_head(head):
        query_block_list = lax.dynamic_slice_in_dim(queries, head * DK, DK, 1).astype(jnp.float32).reshape(block_count, BLOCK, DK)
        key_blocks = lax.dynamic_slice_in_dim(keys, head * DK, DK, 1).astype(jnp.float32).reshape(block_count, BLOCK, DK)
        value_block_list = lax.dynamic_slice_in_dim(values, head * DV, DV, 1).astype(jnp.float32).reshape(block_count, BLOCK, DV)
        gradient_block_list = lax.dynamic_slice_in_dim(grad_out, head * DV, DV, 1).astype(jnp.float32).reshape(block_count, BLOCK, DV)
        log_rates = lax.dynamic_index_in_dim(log_decay, head, 0, keepdims=False)
        weights, per_head_decay_rate, tail_decay, block_decay = decay_tables(log_rates, doc_ids, BLOCK, score_scaling)
        zero_state = jnp.zeros((DK, DV), jnp.float32)
        keyed_blocks = rounded(key_blocks * tail_decay[:, :, None])
        updates = jnp.einsum('ncd,nce->nde', keyed_blocks, value_block_list)
        last_state, states = lax.scan(forward_step, zero_state, (block_decay, updates))
        queried = rounded(query_block_list * (per_head_decay_rate * score_scaling)[:, :, None])
        back_updates = jnp.einsum('ncd,nce->nde', queried, gradient_block_list)
        first_back, ends = lax.scan(forward_step, zero_state, (block_decay, back_updates), reverse=True)
        lowered_state = rounded(states)
        back_low = rounded(ends)
        scores = jnp.einsum('nid,njd->nij', query_block_list, key_blocks)
        attention_weights = rounded(scores * weights)
        retained = jnp.einsum('xho,xoy->xhy', query_block_list, lowered_state) * (per_head_decay_rate * score_scaling)[:, :, None]
        retained = retained + jnp.einsum('bcv,bvd->bcd', attention_weights, value_block_list)
        score_gradient = jnp.einsum('ysb,ytb->yst', gradient_block_list, value_block_list)
        gprobs = rounded(score_gradient * weights)
        query_gradient = jnp.einsum('srj,sqj->srq', gradient_block_list, lowered_state) * (per_head_decay_rate * score_scaling)[:, :, None]
        query_gradient = query_gradient + jnp.einsum('nij,njd->nid', gprobs, key_blocks)
        grad_k = jnp.einsum('nje,nde->njd', value_block_list, back_low) * tail_decay[:, :, None]
        grad_k = grad_k + jnp.einsum('nij,nid->njd', gprobs, query_block_list)
        value_gradient = jnp.einsum('njd,nde->nje', key_blocks, back_low) * tail_decay[:, :, None]
        value_gradient = value_gradient + jnp.einsum('glu,glx->gux', attention_weights, gradient_block_list)
        return (retained.reshape(WINDOW_TOKENS, DV).astype(jnp.bfloat16), query_gradient.reshape(WINDOW_TOKENS, DK).astype(jnp.bfloat16),
                grad_k.reshape(WINDOW_TOKENS, DK).astype(jnp.bfloat16), value_gradient.reshape(WINDOW_TOKENS, DV).astype(jnp.bfloat16))

    stacked = lax.map(one_head, jnp.arange(HEADS, dtype=jnp.int32))

    def merge_heads(per_head):
        return jnp.transpose(per_head, (1, 0, 2)).reshape(WINDOW_TOKENS, -1)

    return (merge_heads(stacked[0]), merge_heads(stacked[1]), merge_heads(stacked[2]), merge_heads(stacked[3]))
```

```python
import jax
import jax.numpy as jnp
import functools

from jax import lax
from jax.experimental import pallas as pl
from jax.experimental.pallas import tpu as pltpu
from jax.sharding import PartitionSpec as P

BLOCK = 128


def passed_along(block, axis, distance):
    devices = range(lax.axis_size(axis))
    route = [(i - distance, i) for i in devices if i - distance in devices]
    return lax.ppermute(block, axis, route)


def document_ids(doc_lengths, first_place, span_length):
    starts = jnp.cumsum(doc_lengths, dtype=jnp.int32) - doc_lengths
    places = first_place - 1 + jnp.arange(span_length + 1, dtype=jnp.int32)
    return jnp.sum((starts[None, :] <= places[:, None]).astype(jnp.int32), axis=1) - 1


def decay_tables(log_rates, doc_ids, block_size, score_scaling):
    block_count = log_rates.shape[0] // block_size
    cumulated = jnp.cumsum(log_rates.reshape(block_count, block_size), axis=1)
    before = doc_ids[0 : block_count * block_size : block_size]
    own_ids = doc_ids[1:].reshape(block_count, block_size)
    carried = (own_ids == before[:, None]).astype(jnp.float32)
    last_ids = own_ids[:, block_size - 1]
    tail_mask = (own_ids == last_ids[:, None]).astype(jnp.float32)
    block_decay = jnp.exp(cumulated[:, block_size - 1]) * carried[:, block_size - 1]
    row_index = lax.broadcasted_iota(jnp.int32, (block_size, block_size), 0)
    column_index = lax.broadcasted_iota(jnp.int32, (block_size, block_size), 1)
    inside = (own_ids[:, :, None] == own_ids[:, None, :]) & (row_index >= column_index)[None]
    decay_gaps = cumulated[:, :, None] - cumulated[:, None, :]
    weights = jnp.where(inside, jnp.exp(jnp.where(inside, decay_gaps, 0.0)), 0.0) * score_scaling
    per_head_decay_rate = jnp.exp(cumulated) * carried
    tail_decay = jnp.exp(cumulated[:, block_size - 1 :] - cumulated) * tail_mask
    return (weights, per_head_decay_rate, tail_decay, block_decay)


def chain_combine(earlier, follower):
    return (earlier[0] * follower[0], follower[0] * earlier[1] + follower[1])


def offset_list(shard_total):
    return [1] + [1 << level for level in range((shard_total - 1).bit_length())]


def per_device(queries, keys, values, grad_out, log_decay, doc_lengths):
    query_rows, key_rows, value_rows = (
        lax.all_to_all(queries, "head", split_axis=1, concat_axis=0, tiled=True),
        lax.all_to_all(keys, "head", split_axis=1, concat_axis=0, tiled=True),
        lax.all_to_all(values, "head", split_axis=1, concat_axis=0, tiled=True),
    )
    tok_dev, key_dim = key_rows.shape
    value_dim = value_rows.shape[1]
    block_count = tok_dev // BLOCK
    score_scaling = (key_dim * BLOCK) ** (-0.5)
    shard_total = lax.axis_size("ctx")
    doc_ids = document_ids(doc_lengths, lax.axis_index("ctx") * tok_dev, tok_dev)
    weights, per_head_decay_rate, tail_decay, block_decay = decay_tables(
        log_decay[0], doc_ids, BLOCK, score_scaling
    )
    query_block_list = query_rows.reshape(block_count, BLOCK, key_dim)
    key_blocks = key_rows.reshape(block_count, BLOCK, key_dim)
    value_block_list = value_rows.reshape(block_count, BLOCK, value_dim)
    gradient_block_list = grad_out.reshape(block_count, BLOCK, value_dim)
    zero_state = jnp.zeros((key_dim, value_dim), jnp.float32)
    keyed_blocks = (key_blocks * tail_decay[:, :, None]).astype(jnp.bfloat16)
    updates = jnp.einsum(
        "ncd,nce->nde", keyed_blocks, value_block_list, preferred_element_type=jnp.float32
    )
    local_starts = []
    running = zero_state
    factor = jnp.float32(1.0)
    block_index = 0
    local_starts.append(running)
    carry_gains = factor
    running = block_decay[block_index] * running + updates[block_index]
    factor = factor * block_decay[block_index]
    shard_decay = factor
    current = (shard_decay, running)
    for position, offset in enumerate(offset_list(shard_total)):
        pulled = passed_along((current[0], current[1]), "ctx", offset)
        current = pulled if position == 0 else chain_combine(pulled, current)
    incoming = current[1]
    states = jnp.stack([carry_gains * incoming])
    queried = (query_block_list * (per_head_decay_rate * score_scaling)[:, :, None]).astype(
        jnp.bfloat16
    )
    back_updates = jnp.einsum(
        "ncd,nce->nde", queried, gradient_block_list, preferred_element_type=jnp.float32
    )
    local_ends = [zero_state] * block_count
    back_gains = [jnp.float32(1.0)] * block_count
    running = zero_state
    factor = jnp.float32(1.0)
    for block_index in reversed(range(block_count)):
        local_ends[block_index] = running
        back_gains[block_index] = factor
        running = block_decay[block_index] * running + back_updates[block_index]
        factor = factor * block_decay[block_index]
    current = (shard_decay, running)
    for position, offset in enumerate(offset_list(shard_total)):
        pulled = passed_along((current[0], current[1]), "ctx", -offset)
        current = pulled if position == 0 else chain_combine(pulled, current)
    arriving = current[1]
    ends = jnp.stack([back_gains[0] * arriving])
    lowered_state = states.astype(jnp.bfloat16)
    back_low = ends.astype(jnp.bfloat16)
    scores = jnp.einsum(
        "nid,njd->nij", query_block_list, key_blocks, preferred_element_type=jnp.float32
    )
    attention_weights = (scores * weights).astype(jnp.bfloat16)
    retained = (
        jnp.einsum(
            "xho,xoy->xhy", query_block_list, lowered_state, preferred_element_type=jnp.float32
        )
        * (per_head_decay_rate * score_scaling)[:, :, None]
    )
    retained = retained + jnp.einsum(
        "bcv,bvd->bcd", attention_weights, value_block_list, preferred_element_type=jnp.float32
    )
    score_gradient = jnp.einsum(
        "ysb,ytb->yst", gradient_block_list, value_block_list, preferred_element_type=jnp.float32
    )
    gprobs = (score_gradient * weights).astype(jnp.bfloat16)
    query_gradient = (
        jnp.einsum(
            "srj,sqj->srq", gradient_block_list, lowered_state, preferred_element_type=jnp.float32
        )
        * (per_head_decay_rate * score_scaling)[:, :, None]
    )
    query_gradient = query_gradient + jnp.einsum(
        "nij,njd->nid", gprobs, key_blocks, preferred_element_type=jnp.float32
    )
    grad_k = (
        jnp.einsum("nje,nde->njd", value_block_list, back_low, preferred_element_type=jnp.float32)
        * tail_decay[:, :, None]
    )
    grad_k = grad_k + jnp.einsum(
        "nij,nid->njd", gprobs, query_block_list, preferred_element_type=jnp.float32
    )
    value_gradient = (
        jnp.einsum("njd,nde->nje", key_blocks, back_low, preferred_element_type=jnp.float32)
        * tail_decay[:, :, None]
    )
    value_gradient = value_gradient + jnp.einsum(
        "glu,glx->gux", attention_weights, gradient_block_list, preferred_element_type=jnp.float32
    )
    return (
        retained.reshape(tok_dev, value_dim).astype(jnp.bfloat16),
        query_gradient.reshape(tok_dev, key_dim).astype(jnp.bfloat16),
        grad_k.reshape(tok_dev, key_dim).astype(jnp.bfloat16),
        value_gradient.reshape(tok_dev, value_dim).astype(jnp.bfloat16),
    )


CHUNKS = 4
MESH = pl.DeviceIdType.MESH
F32, BF16 = jnp.float32, jnp.bfloat16


def dot(left, right, left_dim, right_dim):
    return lax.dot_general(
        left, right, (((left_dim,), (right_dim,)), ((), ())), preferred_element_type=F32
    )


def kernel(
    shards,
    heads,
    q_ref, k_ref, v_ref, g_ref, log_ref, len_ref,
    ret_ref, dq_ref, dk_ref, dv_ref,
    q_all, k_all, v_all, g_all,
    u_buf, w_buf,
    f_first_out, f_first_in, f_state_out, f_state_in,
    b_first_out, b_first_in, b_state_out, b_state_in,
    ret_buf, dq_buf, dk_buf, dv_buf,
    head_send, head_recv, local_sem, out_sem,
    f_first_send, f_first_recv, f_state_send, f_state_recv,
    b_first_send, b_first_recv, b_state_send, b_state_recv,
):
    c, h = lax.axis_index("ctx"), lax.axis_index("head")
    rows = q_ref.shape[0]
    tokens, key_dim = q_all.shape
    value_dim = v_all.shape[1]
    scale = (key_dim * BLOCK) ** -0.5
    even = lax.rem(c, 2) == 0
    odd = jnp.logical_not(even)
    has_earlier, has_later = c > 0, c < shards - 1

    def row_span(head):
        return pl.ds(pl.multiple_of(head * rows, rows), rows)

    def head_copy(number, offset, source_head, target_head, place_head):
        source, gathered = ((q_ref, q_all), (k_ref, k_all), (v_ref, v_all))[number]
        width = gathered.shape[1]
        columns = pl.ds(pl.multiple_of(target_head * width, width), width)
        return source.at[:, columns], gathered.at[row_span(place_head)]

    locals_ = [pltpu.make_async_copy(g_ref, g_all, local_sem.at[3])]
    for number in range(3):
        source, target = head_copy(number, 0, h, h, h)
        locals_.append(pltpu.make_async_copy(source, target, local_sem.at[number]))
    for copy in locals_:
        copy.start()
    local_g, local_parts = locals_[0], locals_[1:]

    barrier = pltpu.get_barrier_semaphore()
    for offset in range(1, heads):
        pl.semaphore_signal(
            barrier, inc=1, device_id=(c, lax.rem(h + offset, heads)), device_id_type=MESH
        )

    @pl.when(has_earlier)
    def _():
        pl.semaphore_signal(barrier, inc=1, device_id=(c - 1, h), device_id_type=MESH)

    @pl.when(has_later)
    def _():
        pl.semaphore_signal(barrier, inc=1, device_id=(c + 1, h), device_id_type=MESH)

    pl.semaphore_wait(
        barrier, heads - 1 + has_earlier.astype(jnp.int32) + has_later.astype(jnp.int32)
    )

    def sent(number, offset):
        peer = lax.rem(h + offset, heads)
        source, target = head_copy(number, offset, h, peer, h)
        return pltpu.make_async_remote_copy(
            src_ref=source, dst_ref=target,
            send_sem=head_send.at[number, offset - 1], recv_sem=head_recv.at[number, offset - 1],
            device_id=(c, peer), device_id_type=MESH,
        )

    def received(number, offset):
        peer = lax.rem(h + heads - offset, heads)
        source, target = head_copy(number, offset, peer, h, peer)
        return pltpu.make_async_remote_copy(
            src_ref=source, dst_ref=target,
            send_sem=head_send.at[number, offset - 1], recv_sem=head_recv.at[number, offset - 1],
            device_id=(c, peer), device_id_type=MESH,
        )

    for number in range(3):
        for offset in range(1, heads):
            sent(number, offset).start()

    def arrived(number):
        local_parts[number].wait()
        for offset in range(1, heads):
            received(number, offset).wait_recv()

    i = lax.broadcasted_iota(jnp.int32, (tokens, tokens), 0)
    j = lax.broadcasted_iota(jnp.int32, (tokens, tokens), 1)
    cum_col = jnp.sum(jnp.where(j <= i, log_ref[...], 0.0), axis=1, keepdims=True)
    cum_row = jnp.sum(jnp.where(i == j, cum_col, 0.0), axis=0, keepdims=True)
    documents = len_ref.shape[1]
    d = lax.broadcasted_iota(jnp.int32, (documents, documents), 0)
    e = lax.broadcasted_iota(jnp.int32, (documents, documents), 1)
    lengths = len_ref[...].astype(F32)
    starts = jnp.sum(jnp.where(e < d, lengths, 0.0), axis=1, keepdims=True)
    first = c * tokens
    places = (lax.broadcasted_iota(jnp.int32, (documents, tokens), 1) + first).astype(F32)
    doc_row = jnp.sum(jnp.where(starts <= places, 1.0, 0.0), axis=0, keepdims=True)
    before_place = (lax.broadcasted_iota(jnp.int32, (documents, 1), 1) + (first - 1)).astype(F32)
    doc_before = jnp.sum(jnp.where(starts <= before_place, 1.0, 0.0), axis=0, keepdims=True)
    doc_col = jnp.sum(jnp.where(i == j, doc_row, 0.0), axis=1, keepdims=True)
    last_lane = lax.broadcasted_iota(jnp.int32, (1, tokens), 1) == tokens - 1
    doc_last = jnp.sum(jnp.where(last_lane, doc_row, 0.0), axis=1, keepdims=True)
    cum_last = jnp.sum(jnp.where(last_lane, cum_row, 0.0), axis=1, keepdims=True)
    inside = (doc_col == doc_row) & (j <= i)
    weights = jnp.where(inside, jnp.exp(jnp.where(inside, cum_col - cum_row, 0.0)), 0.0) * scale
    rate = jnp.where(doc_col == doc_before, jnp.exp(cum_col), 0.0) * scale
    tail = jnp.where(doc_col == doc_last, jnp.exp(cum_last - cum_col), 0.0)
    decay = jnp.where(doc_last == doc_before, jnp.exp(cum_last), 0.0)

    depth = key_dim // CHUNKS

    def passing(update, first_out, first_in, state_out, state_in,
                first_send, first_recv, state_send, state_recv, opens, target, has_source, has_target):
        closes = jnp.logical_not(opens)

        def piece(n):
            return pl.ds(n * depth, depth)

        def first_copy(n):
            return pltpu.make_async_remote_copy(
                src_ref=first_out.at[piece(n)], dst_ref=first_in.at[piece(n)],
                send_sem=first_send.at[n], recv_sem=first_recv.at[n],
                device_id=(target, h), device_id_type=MESH,
            )

        def state_copy(n):
            return pltpu.make_async_remote_copy(
                src_ref=state_out.at[piece(n)], dst_ref=state_in.at[piece(n)],
                send_sem=state_send.at[n], recv_sem=state_recv.at[n],
                device_id=(target, h), device_id_type=MESH,
            )

        def begin():
            @pl.when(opens)
            def _():
                for n in range(CHUNKS):
                    first_out[piece(n), :] = update[piece(n), :].astype(BF16)
                    first_copy(n).start()

            @pl.when(closes & has_target)
            def _():
                for n in range(CHUNKS):
                    first_copy(n).wait_recv()
                    state_out[piece(n), :] = (
                        update[piece(n), :] + decay * first_in[piece(n), :].astype(F32)
                    ).astype(BF16)
                    state_copy(n).start()

            @pl.when(closes & jnp.logical_not(has_target))
            def _():
                for n in range(CHUNKS):
                    first_copy(n).wait_recv()

        def relay():
            @pl.when(opens & jnp.logical_not(has_source))
            def _():
                state_in[...] = jnp.zeros_like(state_in)
                for n in range(CHUNKS):
                    state_out[piece(n), :] = update[piece(n), :].astype(BF16)
                    state_copy(n).start()

            @pl.when(opens & has_source)
            def _():
                for n in range(CHUNKS):
                    state_copy(n).wait_recv()
                    state_out[piece(n), :] = (
                        update[piece(n), :] + decay * state_in[piece(n), :].astype(F32)
                    ).astype(BF16)
                    state_copy(n).start()

            @pl.when(closes)
            def _():
                for n in range(CHUNKS):
                    state_copy(n).wait_recv()

        def finish():
            @pl.when(opens)
            def _():
                for n in range(CHUNKS):
                    first_copy(n).wait_send()

            @pl.when(has_target)
            def _():
                for n in range(CHUNKS):
                    state_copy(n).wait_send()

        return begin, relay, finish

    f_begin, f_relay, f_finish = passing(
        u_buf, f_first_out, f_first_in, f_state_out, f_state_in,
        f_first_send, f_first_recv, f_state_send, f_state_recv,
        even, c + 1, has_earlier, has_later,
    )
    b_begin, b_relay, b_finish = passing(
        w_buf, b_first_out, b_first_in, b_state_out, b_state_in,
        b_first_send, b_first_recv, b_state_send, b_state_recv,
        odd, c - 1, has_later, has_earlier,
    )

    local_g.wait()
    arrived(0)
    g = g_all[...]
    q = q_all[...]
    queried = (q.astype(F32) * rate).astype(BF16)
    w_buf[...] = dot(queried, g, 0, 0)
    b_begin()

    arrived(1)
    arrived(2)
    k, v = k_all[...], v_all[...]
    keyed = (k.astype(F32) * tail).astype(BF16)
    u_buf[...] = dot(keyed, v, 0, 0)
    f_begin()

    probs = (dot(q, k, 1, 1) * weights).astype(BF16)
    gprobs = (dot(g, v, 1, 1) * weights).astype(BF16)
    dk_part = dot(gprobs, q, 0, 0)
    dv_part = dot(probs, g, 0, 0)

    outs = [
        pltpu.make_async_copy(buf, ref, out_sem.at[n])
        for n, (buf, ref) in enumerate(
            ((ret_buf, ret_ref), (dq_buf, dq_ref), (dk_buf, dk_ref), (dv_buf, dv_ref))
        )
    ]
    b_relay()
    back_low = b_state_in[...]
    dk_buf[...] = (dot(v, back_low, 1, 1) * tail + dk_part).astype(BF16)
    outs[2].start()
    dv_buf[...] = (dot(k, back_low, 1, 0) * tail + dv_part).astype(BF16)
    outs[3].start()

    ret_part = dot(probs, v, 1, 0)
    dq_part = dot(gprobs, k, 1, 0)
    f_relay()
    state_low = f_state_in[...]
    ret_buf[...] = (dot(q, state_low, 1, 0) * rate + ret_part).astype(BF16)
    outs[0].start()
    dq_buf[...] = (dot(g, state_low, 1, 1) * rate + dq_part).astype(BF16)
    outs[1].start()

    for number in range(3):
        for offset in range(1, heads):
            sent(number, offset).wait_send()
    b_finish()
    f_finish()
    for copy in outs:
        copy.wait()


def paired(queries, keys, values, grad_out, log_decay, doc_lengths):
    shards, heads = lax.axis_size("ctx"), lax.axis_size("head")
    tokens = queries.shape[0] * heads
    key_dim, value_dim = keys.shape[1] // heads, values.shape[1] // heads
    state = pltpu.VMEM((key_dim, value_dim), BF16)
    total = pltpu.VMEM((key_dim, value_dim), F32)
    narrow, wide = pltpu.VMEM((tokens, key_dim), BF16), pltpu.VMEM((tokens, value_dim), BF16)
    dma = pltpu.SemaphoreType.DMA
    anywhere, vmem = pl.BlockSpec(memory_space=pl.ANY), pl.BlockSpec(memory_space=pltpu.VMEM)
    return tuple(pl.pallas_call(
        functools.partial(kernel, shards, heads),
        out_shape=[
            jax.ShapeDtypeStruct((tokens, value_dim), BF16),
            jax.ShapeDtypeStruct((tokens, key_dim), BF16),
            jax.ShapeDtypeStruct((tokens, key_dim), BF16),
            jax.ShapeDtypeStruct((tokens, value_dim), BF16),
        ],
        in_specs=[anywhere] * 4 + [vmem] * 2,
        out_specs=[anywhere] * 4,
        scratch_shapes=[narrow, narrow, wide, wide, total, total]
        + [state] * 8
        + [wide, narrow, narrow, wide]
        + [dma((3, heads - 1)), dma((3, heads - 1)), dma((4,)), dma((4,))]
        + [dma((CHUNKS,))] * 8,
        compiler_params=pltpu.CompilerParams(
            collective_id=0, has_side_effects=True, vmem_limit_bytes=40 * 1024 * 1024
        ),
    )(queries, keys, values, grad_out, log_decay, doc_lengths.reshape(1, -1)))


def solution(mesh):
    shards, heads = mesh.shape["ctx"], mesh.shape["head"]

    def whole(queries, keys, values, grad_out, log_decay, doc_lengths):
        window = queries.shape[0]
        tokens = window // shards
        reach = -(-(window // 4 - 1) // tokens)
        short = reach <= 2 and shards % 2 == 0 and tokens == BLOCK and (tokens // heads) % 16 == 0
        placed = (
            P(("ctx", "head"), None),
            P(("ctx", "head"), None),
            P(("ctx", "head"), None),
            P("ctx", "head"),
            P("head", "ctx"),
            P(),
        )
        return jax.shard_map(
            paired if short else per_device,
            mesh=mesh,
            in_specs=placed,
            out_specs=(P("ctx", "head"), P("ctx", "head"), P("ctx", "head"), P("ctx", "head")),
            check_vma=False,
        )(queries, keys, values, grad_out, log_decay, doc_lengths)

    return whole
```

```python
import jax
import jax.numpy as jnp
import functools

from jax import lax
from jax.experimental import pallas as pl
from jax.experimental.pallas import tpu as pltpu
from jax.sharding import PartitionSpec as P

BLOCK = 128


def passed_along(block, axis, distance):
    devices = range(lax.axis_size(axis))
    route = [(i - distance, i) for i in devices if i - distance in devices]
    return lax.ppermute(block, axis, route)


def document_ids(doc_lengths, first_place, span_length):
    starts = jnp.cumsum(doc_lengths, dtype=jnp.int32) - doc_lengths
    places = first_place - 1 + jnp.arange(span_length + 1, dtype=jnp.int32)
    return jnp.sum((starts[None, :] <= places[:, None]).astype(jnp.int32), axis=1) - 1


def decay_tables(log_rates, doc_ids, block_size, score_scaling):
    block_count = log_rates.shape[0] // block_size
    cumulated = jnp.cumsum(log_rates.reshape(block_count, block_size), axis=1)
    before = doc_ids[0 : block_count * block_size : block_size]
    own_ids = doc_ids[1:].reshape(block_count, block_size)
    carried = (own_ids == before[:, None]).astype(jnp.float32)
    last_ids = own_ids[:, block_size - 1]
    tail_mask = (own_ids == last_ids[:, None]).astype(jnp.float32)
    block_decay = jnp.exp(cumulated[:, block_size - 1]) * carried[:, block_size - 1]
    row_index = lax.broadcasted_iota(jnp.int32, (block_size, block_size), 0)
    column_index = lax.broadcasted_iota(jnp.int32, (block_size, block_size), 1)
    inside = (own_ids[:, :, None] == own_ids[:, None, :]) & (row_index >= column_index)[None]
    decay_gaps = cumulated[:, :, None] - cumulated[:, None, :]
    weights = jnp.where(inside, jnp.exp(jnp.where(inside, decay_gaps, 0.0)), 0.0) * score_scaling
    per_head_decay_rate = jnp.exp(cumulated) * carried
    tail_decay = jnp.exp(cumulated[:, block_size - 1 :] - cumulated) * tail_mask
    return (weights, per_head_decay_rate, tail_decay, block_decay)


def chain_combine(earlier, follower):
    return (earlier[0] * follower[0], follower[0] * earlier[1] + follower[1])


def offset_list(shard_total):
    return [1] + [1 << level for level in range((shard_total - 1).bit_length())]


def per_device(queries, keys, values, grad_out, log_decay, doc_lengths):
    query_rows, key_rows, value_rows = (
        lax.all_to_all(queries, "head", split_axis=1, concat_axis=0, tiled=True),
        lax.all_to_all(keys, "head", split_axis=1, concat_axis=0, tiled=True),
        lax.all_to_all(values, "head", split_axis=1, concat_axis=0, tiled=True),
    )
    tok_dev, key_dim = key_rows.shape
    value_dim = value_rows.shape[1]
    block_count = tok_dev // BLOCK
    score_scaling = (key_dim * BLOCK) ** (-0.5)
    shard_total = lax.axis_size("ctx")
    doc_ids = document_ids(doc_lengths, lax.axis_index("ctx") * tok_dev, tok_dev)
    weights, per_head_decay_rate, tail_decay, block_decay = decay_tables(
        log_decay[0], doc_ids, BLOCK, score_scaling
    )
    query_block_list = query_rows.reshape(block_count, BLOCK, key_dim)
    key_blocks = key_rows.reshape(block_count, BLOCK, key_dim)
    value_block_list = value_rows.reshape(block_count, BLOCK, value_dim)
    gradient_block_list = grad_out.reshape(block_count, BLOCK, value_dim)
    zero_state = jnp.zeros((key_dim, value_dim), jnp.float32)
    keyed_blocks = (key_blocks * tail_decay[:, :, None]).astype(jnp.bfloat16)
    updates = jnp.einsum(
        "ncd,nce->nde", keyed_blocks, value_block_list, preferred_element_type=jnp.float32
    )
    local_starts = []
    running = zero_state
    factor = jnp.float32(1.0)
    block_index = 0
    local_starts.append(running)
    carry_gains = factor
    running = block_decay[block_index] * running + updates[block_index]
    factor = factor * block_decay[block_index]
    shard_decay = factor
    current = (shard_decay, running)
    for position, offset in enumerate(offset_list(shard_total)):
        pulled = passed_along((current[0], current[1]), "ctx", offset)
        current = pulled if position == 0 else chain_combine(pulled, current)
    incoming = current[1]
    states = jnp.stack([carry_gains * incoming])
    queried = (query_block_list * (per_head_decay_rate * score_scaling)[:, :, None]).astype(
        jnp.bfloat16
    )
    back_updates = jnp.einsum(
        "ncd,nce->nde", queried, gradient_block_list, preferred_element_type=jnp.float32
    )
    local_ends = [zero_state] * block_count
    back_gains = [jnp.float32(1.0)] * block_count
    running = zero_state
    factor = jnp.float32(1.0)
    for block_index in reversed(range(block_count)):
        local_ends[block_index] = running
        back_gains[block_index] = factor
        running = block_decay[block_index] * running + back_updates[block_index]
        factor = factor * block_decay[block_index]
    current = (shard_decay, running)
    for position, offset in enumerate(offset_list(shard_total)):
        pulled = passed_along((current[0], current[1]), "ctx", -offset)
        current = pulled if position == 0 else chain_combine(pulled, current)
    arriving = current[1]
    ends = jnp.stack([back_gains[0] * arriving])
    lowered_state = states.astype(jnp.bfloat16)
    back_low = ends.astype(jnp.bfloat16)
    scores = jnp.einsum(
        "nid,njd->nij", query_block_list, key_blocks, preferred_element_type=jnp.float32
    )
    attention_weights = (scores * weights).astype(jnp.bfloat16)
    retained = (
        jnp.einsum(
            "xho,xoy->xhy", query_block_list, lowered_state, preferred_element_type=jnp.float32
        )
        * (per_head_decay_rate * score_scaling)[:, :, None]
    )
    retained = retained + jnp.einsum(
        "bcv,bvd->bcd", attention_weights, value_block_list, preferred_element_type=jnp.float32
    )
    score_gradient = jnp.einsum(
        "ysb,ytb->yst", gradient_block_list, value_block_list, preferred_element_type=jnp.float32
    )
    gprobs = (score_gradient * weights).astype(jnp.bfloat16)
    query_gradient = (
        jnp.einsum(
            "srj,sqj->srq", gradient_block_list, lowered_state, preferred_element_type=jnp.float32
        )
        * (per_head_decay_rate * score_scaling)[:, :, None]
    )
    query_gradient = query_gradient + jnp.einsum(
        "nij,njd->nid", gprobs, key_blocks, preferred_element_type=jnp.float32
    )
    grad_k = (
        jnp.einsum("nje,nde->njd", value_block_list, back_low, preferred_element_type=jnp.float32)
        * tail_decay[:, :, None]
    )
    grad_k = grad_k + jnp.einsum(
        "nij,nid->njd", gprobs, query_block_list, preferred_element_type=jnp.float32
    )
    value_gradient = (
        jnp.einsum("njd,nde->nje", key_blocks, back_low, preferred_element_type=jnp.float32)
        * tail_decay[:, :, None]
    )
    value_gradient = value_gradient + jnp.einsum(
        "glu,glx->gux", attention_weights, gradient_block_list, preferred_element_type=jnp.float32
    )
    return (
        retained.reshape(tok_dev, value_dim).astype(jnp.bfloat16),
        query_gradient.reshape(tok_dev, key_dim).astype(jnp.bfloat16),
        grad_k.reshape(tok_dev, key_dim).astype(jnp.bfloat16),
        value_gradient.reshape(tok_dev, value_dim).astype(jnp.bfloat16),
    )


CHUNKS = 4
MESH = pl.DeviceIdType.MESH
F32, BF16 = jnp.float32, jnp.bfloat16


def dot(left, right, left_dim, right_dim):
    return lax.dot_general(
        left, right, (((left_dim,), (right_dim,)), ((), ())), preferred_element_type=F32
    )


def kernel(
    shards,
    heads,
    q_ref, k_ref, v_ref, g_ref, log_hbm, len_hbm,
    ret_ref, dq_ref, dk_ref, dv_ref,
    q_all, k_all, v_all, g_all, log_ref, len_ref,
    u_buf, w_buf,
    f_first_out, f_first_in, f_state_out, f_state_in,
    b_first_out, b_first_in, b_state_out, b_state_in,
    ret_part, dq_part, dk_part, dv_part,
    head_send, head_recv, local_sem,
    f_first_send, f_first_recv, f_state_send, f_state_recv,
    b_first_send, b_first_recv, b_state_send, b_state_recv,
):
    c, h = lax.axis_index("ctx"), lax.axis_index("head")
    rows = q_ref.shape[0]
    tokens, key_dim = q_all.shape
    value_dim = v_all.shape[1]
    width = value_dim // CHUNKS
    scale = (key_dim * BLOCK) ** -0.5
    even = lax.rem(c, 2) == 0
    odd = jnp.logical_not(even)
    has_earlier, has_later = c > 0, c < shards - 1

    def columns(n):
        return slice(n * width, (n + 1) * width)

    barrier = pltpu.get_barrier_semaphore()
    for offset in range(1, heads):
        pl.semaphore_signal(
            barrier, inc=1, device_id=(c, lax.rem(h + offset, heads)), device_id_type=MESH
        )

    @pl.when(has_earlier)
    def _():
        pl.semaphore_signal(barrier, inc=1, device_id=(c - 1, h), device_id_type=MESH)

    @pl.when(has_later)
    def _():
        pl.semaphore_signal(barrier, inc=1, device_id=(c + 1, h), device_id_type=MESH)

    def head_copy(number, target_head, place_head):
        if number < 2:
            source, gathered = ((q_ref, q_all), (k_ref, k_all))[number]
            span, place = key_dim, pl.ds(0, key_dim)
            begin = target_head * key_dim
        else:
            source, gathered, span = v_ref, v_all, width
            place = pl.ds((number - 2) * width, width)
            begin = target_head * value_dim + (number - 2) * width
        held = pl.ds(pl.multiple_of(place_head * rows, rows), rows)
        return source.at[:, pl.ds(pl.multiple_of(begin, span), span)], gathered.at[held, place]

    pieces = 2 + CHUNKS
    own = [
        pltpu.make_async_copy(*head_copy(number, h, h), local_sem.at[number])
        for number in range(pieces)
    ]
    small = [
        pltpu.make_async_copy(log_hbm, log_ref, local_sem.at[pieces]),
        pltpu.make_async_copy(len_hbm, len_ref, local_sem.at[pieces + 1]),
    ]
    own_g = pltpu.make_async_copy(g_ref, g_all, local_sem.at[pieces + 2])
    for copy in small + own[:1] + [own_g] + own[1:]:
        copy.start()

    pl.semaphore_wait(
        barrier, heads - 1 + has_earlier.astype(jnp.int32) + has_later.astype(jnp.int32)
    )

    def exchanged(number, offset, incoming):
        peer = lax.rem(h + (heads - offset if incoming else offset), heads)
        source, target = head_copy(number, peer, peer if incoming else h)
        return pltpu.make_async_remote_copy(
            src_ref=source, dst_ref=target,
            send_sem=head_send.at[number, offset - 1], recv_sem=head_recv.at[number, offset - 1],
            device_id=(c, peer), device_id_type=MESH,
        )

    for number in range(pieces):
        for offset in range(1, heads):
            exchanged(number, offset, False).start()

    def arrived(number):
        own[number].wait()
        for offset in range(1, heads):
            exchanged(number, offset, True).wait_recv()

    for copy in small:
        copy.wait()
    i = lax.broadcasted_iota(jnp.int32, (tokens, tokens), 0)
    j = lax.broadcasted_iota(jnp.int32, (tokens, tokens), 1)
    cum_col = jnp.sum(jnp.where(j <= i, log_ref[...], 0.0), axis=1, keepdims=True)
    cum_row = jnp.sum(jnp.where(i == j, cum_col, 0.0), axis=0, keepdims=True)
    documents = len_ref.shape[1]
    d = lax.broadcasted_iota(jnp.int32, (documents, documents), 0)
    e = lax.broadcasted_iota(jnp.int32, (documents, documents), 1)
    lengths = len_ref[...].astype(F32)
    starts = jnp.sum(jnp.where(e < d, lengths, 0.0), axis=1, keepdims=True)
    first = c * tokens
    places = (lax.broadcasted_iota(jnp.int32, (documents, tokens), 1) + first).astype(F32)
    doc_row = jnp.sum(jnp.where(starts <= places, 1.0, 0.0), axis=0, keepdims=True)
    before_place = (lax.broadcasted_iota(jnp.int32, (documents, 1), 1) + (first - 1)).astype(F32)
    doc_before = jnp.sum(jnp.where(starts <= before_place, 1.0, 0.0), axis=0, keepdims=True)
    doc_col = jnp.sum(jnp.where(i == j, doc_row, 0.0), axis=1, keepdims=True)
    last_lane = lax.broadcasted_iota(jnp.int32, (1, tokens), 1) == tokens - 1
    doc_last = jnp.sum(jnp.where(last_lane, doc_row, 0.0), axis=1, keepdims=True)
    cum_last = jnp.sum(jnp.where(last_lane, cum_row, 0.0), axis=1, keepdims=True)
    inside = (doc_col == doc_row) & (j <= i)
    weights = jnp.where(inside, jnp.exp(jnp.where(inside, cum_col - cum_row, 0.0)), 0.0) * scale
    rate = jnp.where(doc_col == doc_before, jnp.exp(cum_col), 0.0) * scale
    tail = jnp.where(doc_col == doc_last, jnp.exp(cum_last - cum_col), 0.0)
    decay = jnp.where(doc_last == doc_before, jnp.exp(cum_last), 0.0)

    def passing(update, first_out, first_in, state_out, state_in,
                first_send, first_recv, state_send, state_recv, opens, target, has_source, has_target):
        closes = jnp.logical_not(opens)

        def first_copy(n):
            return pltpu.make_async_remote_copy(
                src_ref=first_out.at[n], dst_ref=first_in.at[n],
                send_sem=first_send.at[n], recv_sem=first_recv.at[n],
                device_id=(target, h), device_id_type=MESH,
            )

        def state_copy(n):
            return pltpu.make_async_remote_copy(
                src_ref=state_out.at[n], dst_ref=state_in.at[n],
                send_sem=state_send.at[n], recv_sem=state_recv.at[n],
                device_id=(target, h), device_id_type=MESH,
            )

        def open_pair(n):
            @pl.when(opens)
            def _():
                first_out[n] = update[n].astype(BF16)
                first_copy(n).start()

        def close_pair():
            @pl.when(closes)
            def _():
                for n in range(CHUNKS):
                    close_chunk(n)

        def close_chunk(n):
            first_copy(n).wait_recv()

            @pl.when(has_target)
            def _():
                state_out[n] = (update[n] + decay * first_in[n].astype(F32)).astype(BF16)
                state_copy(n).start()

        def relay(n):
            @pl.when(has_source)
            def _():
                state_copy(n).wait_recv()

            @pl.when(jnp.logical_not(has_source))
            def _():
                state_in[n] = jnp.zeros(state_in.shape[1:], BF16)

            @pl.when(opens)
            def _():
                state_out[n] = (update[n] + decay * state_in[n].astype(F32)).astype(BF16)
                state_copy(n).start()

        def finish():
            @pl.when(opens)
            def _():
                for n in range(CHUNKS):
                    first_copy(n).wait_send()

            @pl.when(has_target)
            def _():
                for n in range(CHUNKS):
                    state_copy(n).wait_send()

        return open_pair, close_pair, close_chunk, relay, finish

    f_open, _, f_close_chunk, f_relay, f_finish = passing(
        u_buf, f_first_out, f_first_in, f_state_out, f_state_in,
        f_first_send, f_first_recv, f_state_send, f_state_recv,
        even, c + 1, has_earlier, has_later,
    )
    b_open, b_close, _, b_relay, b_finish = passing(
        w_buf, b_first_out, b_first_in, b_state_out, b_state_in,
        b_first_send, b_first_recv, b_state_send, b_state_recv,
        odd, c - 1, has_later, has_earlier,
    )

    own_g.wait()
    arrived(0)
    queried = (q_all[...].astype(F32) * rate).astype(BF16)
    for n in range(CHUNKS):
        w_buf[n] = dot(queried, g_all[:, columns(n)], 0, 0)
        b_open(n)
    b_close()

    arrived(1)
    keyed = (k_all[...].astype(F32) * tail).astype(BF16)
    probs = (dot(q_all[...], k_all[...], 1, 1) * weights).astype(BF16)
    dv_part[...] = dot(probs, g_all[...], 0, 0)
    for n in range(CHUNKS):
        arrived(2 + n)
        u_buf[n] = dot(keyed, v_all[:, columns(n)], 0, 0)
        f_open(n)
        if n:
            pl.when(odd)(functools.partial(f_close_chunk, n - 1))
    pl.when(odd)(functools.partial(f_close_chunk, CHUNKS - 1))

    gprobs = (dot(g_all[...], v_all[...], 1, 1) * weights).astype(BF16)
    dk_part[...] = dot(gprobs, q_all[...], 0, 0)
    dq_part[...] = dot(gprobs, k_all[...], 1, 0)
    ret_part[...] = dot(probs, v_all[...], 1, 0)

    total = jnp.zeros((tokens, key_dim), F32)
    for n in range(CHUNKS):
        b_relay(n)
        back = b_state_in[n]
        dv_ref[:, columns(n)] = (
            dot(k_all[...], back, 1, 0) * tail + dv_part[:, columns(n)]
        ).astype(BF16)
        total += dot(v_all[:, columns(n)], back, 1, 1)
    dk_ref[...] = (total * tail + dk_part[...]).astype(BF16)

    total = jnp.zeros((tokens, key_dim), F32)
    for n in range(CHUNKS):
        f_relay(n)
        state = f_state_in[n]
        ret_ref[:, columns(n)] = (
            dot(q_all[...], state, 1, 0) * rate + ret_part[:, columns(n)]
        ).astype(BF16)
        total += dot(g_all[:, columns(n)], state, 1, 1)
    dq_ref[...] = (total * rate + dq_part[...]).astype(BF16)

    for number in range(pieces):
        for offset in range(1, heads):
            exchanged(number, offset, False).wait_send()
    b_finish()
    f_finish()


def leave(*refs):
    count = len(refs) // 2
    sem = refs[-1]
    copies = [
        pltpu.make_async_copy(refs[n], refs[count + n], sem.at[n]) for n in range(count)
    ]
    for copy in copies:
        copy.start()
    for copy in copies:
        copy.wait()


def paired(queries, keys, values, grad_out, log_decay, doc_lengths):
    shards, heads = lax.axis_size("ctx"), lax.axis_size("head")
    tokens = queries.shape[0] * heads
    key_dim, value_dim = keys.shape[1] // heads, values.shape[1] // heads
    state = pltpu.VMEM((CHUNKS, key_dim, value_dim // CHUNKS), BF16)
    total = pltpu.VMEM((CHUNKS, key_dim, value_dim // CHUNKS), F32)
    dma = pltpu.SemaphoreType.DMA
    hbm, vmem = pl.BlockSpec(memory_space=pltpu.HBM), pl.BlockSpec(memory_space=pltpu.VMEM)
    wides = (value_dim, key_dim, key_dim, value_dim)
    outs = [jax.ShapeDtypeStruct((tokens, width), BF16) for width in wides]
    lengths = doc_lengths.reshape(1, -1)
    results = pl.pallas_call(
        functools.partial(kernel, shards, heads),
        out_shape=outs,
        in_specs=[hbm] * 6,
        out_specs=[vmem] * 4,
        scratch_shapes=[
            pltpu.VMEM((tokens, width), BF16) for width in (key_dim, key_dim, value_dim, value_dim)
        ]
        + [pltpu.VMEM(log_decay.shape, F32), pltpu.VMEM(lengths.shape, jnp.int32)]
        + [total] * 2
        + [state] * 8
        + [pltpu.VMEM((tokens, width), F32) for width in wides]
        + [dma((2 + CHUNKS, heads - 1)), dma((2 + CHUNKS, heads - 1)), dma((5 + CHUNKS,))]
        + [dma((CHUNKS,))] * 8,
        compiler_params=pltpu.CompilerParams(
            collective_id=0, has_side_effects=True, vmem_limit_bytes=40 * 1024 * 1024
        ),
    )(*[
        pltpu.with_memory_space_constraint(x, pltpu.HBM)
        for x in (queries, keys, values, grad_out, log_decay, lengths)
    ])
    return tuple(pl.pallas_call(
        leave,
        out_shape=outs,
        in_specs=[vmem] * 4,
        out_specs=[hbm] * 4,
        scratch_shapes=[dma((4,))],
    )(*results))


def solution(mesh):
    shards, heads = mesh.shape["ctx"], mesh.shape["head"]

    def whole(queries, keys, values, grad_out, log_decay, doc_lengths):
        window = queries.shape[0]
        tokens = window // shards
        reach = -(-(window // 4 - 1) // tokens)
        short = reach <= 2 and shards % 2 == 0 and tokens == BLOCK and (tokens // heads) % 16 == 0
        placed = (
            P(("ctx", "head"), None),
            P(("ctx", "head"), None),
            P(("ctx", "head"), None),
            P("ctx", "head"),
            P("head", "ctx"),
            P(),
        )
        return jax.shard_map(
            paired if short else per_device,
            mesh=mesh,
            in_specs=placed,
            out_specs=(P("ctx", "head"), P("ctx", "head"), P("ctx", "head"), P("ctx", "head")),
            check_vma=False,
        )(queries, keys, values, grad_out, log_decay, doc_lengths)

    return whole
```

```python
import jax
import jax.numpy as jnp
import functools

from jax import lax
from jax.experimental import pallas as pl
from jax.experimental.pallas import tpu as pltpu
from jax.sharding import PartitionSpec as P

BLOCK = 128


def passed_along(block, axis, distance):
    devices = range(lax.axis_size(axis))
    route = [(i - distance, i) for i in devices if i - distance in devices]
    return lax.ppermute(block, axis, route)


def document_ids(doc_lengths, first_place, span_length):
    starts = jnp.cumsum(doc_lengths, dtype=jnp.int32) - doc_lengths
    places = first_place - 1 + jnp.arange(span_length + 1, dtype=jnp.int32)
    return jnp.sum((starts[None, :] <= places[:, None]).astype(jnp.int32), axis=1) - 1


def decay_tables(log_rates, doc_ids, block_size, score_scaling):
    block_count = log_rates.shape[0] // block_size
    cumulated = jnp.cumsum(log_rates.reshape(block_count, block_size), axis=1)
    before = doc_ids[0 : block_count * block_size : block_size]
    own_ids = doc_ids[1:].reshape(block_count, block_size)
    carried = (own_ids == before[:, None]).astype(jnp.float32)
    last_ids = own_ids[:, block_size - 1]
    tail_mask = (own_ids == last_ids[:, None]).astype(jnp.float32)
    block_decay = jnp.exp(cumulated[:, block_size - 1]) * carried[:, block_size - 1]
    row_index = lax.broadcasted_iota(jnp.int32, (block_size, block_size), 0)
    column_index = lax.broadcasted_iota(jnp.int32, (block_size, block_size), 1)
    inside = (own_ids[:, :, None] == own_ids[:, None, :]) & (row_index >= column_index)[None]
    decay_gaps = cumulated[:, :, None] - cumulated[:, None, :]
    weights = jnp.where(inside, jnp.exp(jnp.where(inside, decay_gaps, 0.0)), 0.0) * score_scaling
    per_head_decay_rate = jnp.exp(cumulated) * carried
    tail_decay = jnp.exp(cumulated[:, block_size - 1 :] - cumulated) * tail_mask
    return (weights, per_head_decay_rate, tail_decay, block_decay)


def chain_combine(earlier, follower):
    return (earlier[0] * follower[0], follower[0] * earlier[1] + follower[1])


def offset_list(shard_total):
    return [1] + [1 << level for level in range((shard_total - 1).bit_length())]


def per_device(queries, keys, values, grad_out, log_decay, doc_lengths):
    query_rows, key_rows, value_rows = (
        lax.all_to_all(queries, "head", split_axis=1, concat_axis=0, tiled=True),
        lax.all_to_all(keys, "head", split_axis=1, concat_axis=0, tiled=True),
        lax.all_to_all(values, "head", split_axis=1, concat_axis=0, tiled=True),
    )
    tok_dev, key_dim = key_rows.shape
    value_dim = value_rows.shape[1]
    block_count = tok_dev // BLOCK
    score_scaling = (key_dim * BLOCK) ** (-0.5)
    shard_total = lax.axis_size("ctx")
    doc_ids = document_ids(doc_lengths, lax.axis_index("ctx") * tok_dev, tok_dev)
    weights, per_head_decay_rate, tail_decay, block_decay = decay_tables(
        log_decay[0], doc_ids, BLOCK, score_scaling
    )
    query_block_list = query_rows.reshape(block_count, BLOCK, key_dim)
    key_blocks = key_rows.reshape(block_count, BLOCK, key_dim)
    value_block_list = value_rows.reshape(block_count, BLOCK, value_dim)
    gradient_block_list = grad_out.reshape(block_count, BLOCK, value_dim)
    zero_state = jnp.zeros((key_dim, value_dim), jnp.float32)
    keyed_blocks = (key_blocks * tail_decay[:, :, None]).astype(jnp.bfloat16)
    updates = jnp.einsum(
        "ncd,nce->nde", keyed_blocks, value_block_list, preferred_element_type=jnp.float32
    )
    local_starts = []
    running = zero_state
    factor = jnp.float32(1.0)
    block_index = 0
    local_starts.append(running)
    carry_gains = factor
    running = block_decay[block_index] * running + updates[block_index]
    factor = factor * block_decay[block_index]
    shard_decay = factor
    current = (shard_decay, running)
    for position, offset in enumerate(offset_list(shard_total)):
        pulled = passed_along((current[0], current[1]), "ctx", offset)
        current = pulled if position == 0 else chain_combine(pulled, current)
    incoming = current[1]
    states = jnp.stack([carry_gains * incoming])
    queried = (query_block_list * (per_head_decay_rate * score_scaling)[:, :, None]).astype(
        jnp.bfloat16
    )
    back_updates = jnp.einsum(
        "ncd,nce->nde", queried, gradient_block_list, preferred_element_type=jnp.float32
    )
    local_ends = [zero_state] * block_count
    back_gains = [jnp.float32(1.0)] * block_count
    running = zero_state
    factor = jnp.float32(1.0)
    for block_index in reversed(range(block_count)):
        local_ends[block_index] = running
        back_gains[block_index] = factor
        running = block_decay[block_index] * running + back_updates[block_index]
        factor = factor * block_decay[block_index]
    current = (shard_decay, running)
    for position, offset in enumerate(offset_list(shard_total)):
        pulled = passed_along((current[0], current[1]), "ctx", -offset)
        current = pulled if position == 0 else chain_combine(pulled, current)
    arriving = current[1]
    ends = jnp.stack([back_gains[0] * arriving])
    lowered_state = states.astype(jnp.bfloat16)
    back_low = ends.astype(jnp.bfloat16)
    scores = jnp.einsum(
        "nid,njd->nij", query_block_list, key_blocks, preferred_element_type=jnp.float32
    )
    attention_weights = (scores * weights).astype(jnp.bfloat16)
    retained = (
        jnp.einsum(
            "xho,xoy->xhy", query_block_list, lowered_state, preferred_element_type=jnp.float32
        )
        * (per_head_decay_rate * score_scaling)[:, :, None]
    )
    retained = retained + jnp.einsum(
        "bcv,bvd->bcd", attention_weights, value_block_list, preferred_element_type=jnp.float32
    )
    score_gradient = jnp.einsum(
        "ysb,ytb->yst", gradient_block_list, value_block_list, preferred_element_type=jnp.float32
    )
    gprobs = (score_gradient * weights).astype(jnp.bfloat16)
    query_gradient = (
        jnp.einsum(
            "srj,sqj->srq", gradient_block_list, lowered_state, preferred_element_type=jnp.float32
        )
        * (per_head_decay_rate * score_scaling)[:, :, None]
    )
    query_gradient = query_gradient + jnp.einsum(
        "nij,njd->nid", gprobs, key_blocks, preferred_element_type=jnp.float32
    )
    grad_k = (
        jnp.einsum("nje,nde->njd", value_block_list, back_low, preferred_element_type=jnp.float32)
        * tail_decay[:, :, None]
    )
    grad_k = grad_k + jnp.einsum(
        "nij,nid->njd", gprobs, query_block_list, preferred_element_type=jnp.float32
    )
    value_gradient = (
        jnp.einsum("njd,nde->nje", key_blocks, back_low, preferred_element_type=jnp.float32)
        * tail_decay[:, :, None]
    )
    value_gradient = value_gradient + jnp.einsum(
        "glu,glx->gux", attention_weights, gradient_block_list, preferred_element_type=jnp.float32
    )
    return (
        retained.reshape(tok_dev, value_dim).astype(jnp.bfloat16),
        query_gradient.reshape(tok_dev, key_dim).astype(jnp.bfloat16),
        grad_k.reshape(tok_dev, key_dim).astype(jnp.bfloat16),
        value_gradient.reshape(tok_dev, value_dim).astype(jnp.bfloat16),
    )


CHUNKS = 4
PARTS = 2
MESH = pl.DeviceIdType.MESH
F32, BF16 = jnp.float32, jnp.bfloat16


def dot(left, right, left_dim, right_dim):
    return lax.dot_general(
        left, right, (((left_dim,), (right_dim,)), ((), ())), preferred_element_type=F32
    )


def kernel(
    shards,
    heads,
    q_ref, k_ref, v_ref, g_ref, log_hbm, len_hbm,
    ret_ref, dq_ref, dk_ref, dv_ref,
    q_all, k_all, v_all, g_all, log_ref, len_ref,
    u_buf, w_buf,
    f_first_out, f_first_in, f_state_out, f_state_in,
    b_first_out, b_first_in, b_state_out, b_state_in,
    ret_part, dq_part, dk_part, dv_part,
    head_send, head_recv, local_sem,
    f_first_send, f_first_recv, f_state_send, f_state_recv,
    b_first_send, b_first_recv, b_state_send, b_state_recv,
):
    c, h = lax.axis_index("ctx"), lax.axis_index("head")
    rows = q_ref.shape[0]
    tokens, key_dim = q_all.shape
    value_dim = v_all.shape[1]
    width = value_dim // CHUNKS
    part = value_dim // PARTS
    scale = (key_dim * BLOCK) ** -0.5
    even = lax.rem(c, 2) == 0
    odd = jnp.logical_not(even)
    has_earlier, has_later = c > 0, c < shards - 1

    def columns(n):
        return slice(n * width, (n + 1) * width)

    barrier = pltpu.get_barrier_semaphore()
    for offset in range(1, heads):
        pl.semaphore_signal(
            barrier, inc=1, device_id=(c, lax.rem(h + offset, heads)), device_id_type=MESH
        )

    @pl.when(has_earlier)
    def _():
        pl.semaphore_signal(barrier, inc=1, device_id=(c - 1, h), device_id_type=MESH)

    @pl.when(has_later)
    def _():
        pl.semaphore_signal(barrier, inc=1, device_id=(c + 1, h), device_id_type=MESH)

    def head_copy(number, target_head, place_head):
        if number < 2:
            source, gathered = ((q_ref, q_all), (k_ref, k_all))[number]
            span, place = key_dim, pl.ds(0, key_dim)
            begin = target_head * key_dim
        else:
            source, gathered, span = v_ref, v_all, part
            place = pl.ds((number - 2) * part, part)
            begin = target_head * value_dim + (number - 2) * part
        held = pl.ds(pl.multiple_of(place_head * rows, rows), rows)
        return source.at[:, pl.ds(pl.multiple_of(begin, span), span)], gathered.at[held, place]

    pieces = 2 + PARTS
    own = [
        pltpu.make_async_copy(*head_copy(number, h, h), local_sem.at[number])
        for number in range(pieces)
    ]
    small = [
        pltpu.make_async_copy(log_hbm, log_ref, local_sem.at[pieces]),
        pltpu.make_async_copy(len_hbm, len_ref, local_sem.at[pieces + 1]),
    ]
    own_g = pltpu.make_async_copy(g_ref, g_all, local_sem.at[pieces + 2])
    for copy in small + own[:1] + [own_g] + own[1:]:
        copy.start()

    pl.semaphore_wait(
        barrier, heads - 1 + has_earlier.astype(jnp.int32) + has_later.astype(jnp.int32)
    )

    def exchanged(number, offset, incoming):
        peer = lax.rem(h + (heads - offset if incoming else offset), heads)
        source, target = head_copy(number, peer, peer if incoming else h)
        return pltpu.make_async_remote_copy(
            src_ref=source, dst_ref=target,
            send_sem=head_send.at[number, offset - 1], recv_sem=head_recv.at[number, offset - 1],
            device_id=(c, peer), device_id_type=MESH,
        )

    for offset in range(1, heads):
        exchanged(0, offset, False).start()

    def arrived(number):
        own[number].wait()
        for offset in range(1, heads):
            exchanged(number, offset, True).wait_recv()

    for copy in small:
        copy.wait()
    i = lax.broadcasted_iota(jnp.int32, (tokens, tokens), 0)
    j = lax.broadcasted_iota(jnp.int32, (tokens, tokens), 1)
    cum_col = jnp.sum(jnp.where(j <= i, log_ref[...], 0.0), axis=1, keepdims=True)
    cum_row = jnp.sum(jnp.where(i == j, cum_col, 0.0), axis=0, keepdims=True)
    documents = len_ref.shape[1]
    d = lax.broadcasted_iota(jnp.int32, (documents, documents), 0)
    e = lax.broadcasted_iota(jnp.int32, (documents, documents), 1)
    lengths = len_ref[...].astype(F32)
    starts = jnp.sum(jnp.where(e < d, lengths, 0.0), axis=1, keepdims=True)
    first = c * tokens
    places = (lax.broadcasted_iota(jnp.int32, (documents, tokens), 1) + first).astype(F32)
    doc_row = jnp.sum(jnp.where(starts <= places, 1.0, 0.0), axis=0, keepdims=True)
    before_place = (lax.broadcasted_iota(jnp.int32, (documents, 1), 1) + (first - 1)).astype(F32)
    doc_before = jnp.sum(jnp.where(starts <= before_place, 1.0, 0.0), axis=0, keepdims=True)
    doc_col = jnp.sum(jnp.where(i == j, doc_row, 0.0), axis=1, keepdims=True)
    last_lane = lax.broadcasted_iota(jnp.int32, (1, tokens), 1) == tokens - 1
    doc_last = jnp.sum(jnp.where(last_lane, doc_row, 0.0), axis=1, keepdims=True)
    cum_last = jnp.sum(jnp.where(last_lane, cum_row, 0.0), axis=1, keepdims=True)
    inside = (doc_col == doc_row) & (j <= i)
    weights = jnp.where(inside, jnp.exp(jnp.where(inside, cum_col - cum_row, 0.0)), 0.0) * scale
    rate = jnp.where(doc_col == doc_before, jnp.exp(cum_col), 0.0) * scale
    tail = jnp.where(doc_col == doc_last, jnp.exp(cum_last - cum_col), 0.0)
    decay = jnp.where(doc_last == doc_before, jnp.exp(cum_last), 0.0)

    for number in range(1, pieces):
        for offset in range(1, heads):
            exchanged(number, offset, False).start()

    def passing(update, first_out, first_in, state_out, state_in,
                first_send, first_recv, state_send, state_recv, opens, target, has_source, has_target):
        closes = jnp.logical_not(opens)

        def first_copy(n):
            return pltpu.make_async_remote_copy(
                src_ref=first_out.at[n], dst_ref=first_in.at[n],
                send_sem=first_send.at[n], recv_sem=first_recv.at[n],
                device_id=(target, h), device_id_type=MESH,
            )

        def state_copy(n):
            return pltpu.make_async_remote_copy(
                src_ref=state_out.at[n], dst_ref=state_in.at[n],
                send_sem=state_send.at[n], recv_sem=state_recv.at[n],
                device_id=(target, h), device_id_type=MESH,
            )

        def open_pair(n):
            @pl.when(opens)
            def _():
                first_out[n] = update[n].astype(BF16)
                first_copy(n).start()

        def close_pair():
            @pl.when(closes)
            def _():
                for n in range(CHUNKS):
                    close_chunk(n)

        def close_chunk(n):
            first_copy(n).wait_recv()

            @pl.when(has_target)
            def _():
                state_out[n] = (update[n] + decay * first_in[n].astype(F32)).astype(BF16)
                state_copy(n).start()

        def relay(n):
            @pl.when(has_source)
            def _():
                state_copy(n).wait_recv()

            @pl.when(jnp.logical_not(has_source))
            def _():
                state_in[n] = jnp.zeros(state_in.shape[1:], BF16)

            @pl.when(opens)
            def _():
                state_out[n] = (update[n] + decay * state_in[n].astype(F32)).astype(BF16)
                state_copy(n).start()

        def finish():
            @pl.when(opens)
            def _():
                for n in range(CHUNKS):
                    first_copy(n).wait_send()

            @pl.when(has_target)
            def _():
                for n in range(CHUNKS):
                    state_copy(n).wait_send()

        return open_pair, close_pair, close_chunk, relay, finish

    f_open, _, f_close_chunk, f_relay, f_finish = passing(
        u_buf, f_first_out, f_first_in, f_state_out, f_state_in,
        f_first_send, f_first_recv, f_state_send, f_state_recv,
        even, c + 1, has_earlier, has_later,
    )
    b_open, b_close, _, b_relay, b_finish = passing(
        w_buf, b_first_out, b_first_in, b_state_out, b_state_in,
        b_first_send, b_first_recv, b_state_send, b_state_recv,
        odd, c - 1, has_later, has_earlier,
    )

    own_g.wait()
    arrived(0)
    queried = (q_all[...].astype(F32) * rate).T.astype(BF16)
    for n in range(CHUNKS):
        w_buf[n] = dot(queried, g_all[:, columns(n)], 1, 0)
        b_open(n)
    b_close()

    arrived(1)
    keyed = (k_all[...].astype(F32) * tail).T.astype(BF16)
    probs = (dot(q_all[...], k_all[...], 1, 1) * weights).astype(BF16)
    dv_part[...] = dot(probs, g_all[...], 0, 0)
    for n in range(CHUNKS):
        if n % (CHUNKS // PARTS) == 0:
            arrived(2 + n // (CHUNKS // PARTS))
        u_buf[n] = dot(keyed, v_all[:, columns(n)], 1, 0)
        f_open(n)
        if n:
            pl.when(odd)(functools.partial(f_close_chunk, n - 1))
    pl.when(odd)(functools.partial(f_close_chunk, CHUNKS - 1))

    gprobs = (dot(g_all[...], v_all[...], 1, 1) * weights).astype(BF16)
    dk_part[...] = dot(gprobs, q_all[...], 0, 0)
    dq_part[...] = dot(gprobs, k_all[...], 1, 0)
    ret_part[...] = dot(probs, v_all[...], 1, 0)

    total = jnp.zeros((tokens, key_dim), F32)
    for n in range(CHUNKS):
        b_relay(n)
        back = b_state_in[n]
        dv_ref[:, columns(n)] = (
            dot(k_all[...], back, 1, 0) * tail + dv_part[:, columns(n)]
        ).astype(BF16)
        total += dot(v_all[:, columns(n)], back, 1, 1)
    dk_ref[...] = (total * tail + dk_part[...]).astype(BF16)

    total = jnp.zeros((tokens, key_dim), F32)
    for n in range(CHUNKS):
        f_relay(n)
        state = f_state_in[n]
        ret_ref[:, columns(n)] = (
            dot(q_all[...], state, 1, 0) * rate + ret_part[:, columns(n)]
        ).astype(BF16)
        total += dot(g_all[:, columns(n)], state, 1, 1)
    dq_ref[...] = (total * rate + dq_part[...]).astype(BF16)

    for number in range(pieces):
        for offset in range(1, heads):
            exchanged(number, offset, False).wait_send()
    b_finish()
    f_finish()


def leave(*refs):
    count = len(refs) // 2
    sem = refs[-1]
    copies = [
        pltpu.make_async_copy(refs[n], refs[count + n], sem.at[n]) for n in range(count)
    ]
    for copy in copies:
        copy.start()
    for copy in copies:
        copy.wait()


def paired(queries, keys, values, grad_out, log_decay, doc_lengths):
    shards, heads = lax.axis_size("ctx"), lax.axis_size("head")
    tokens = queries.shape[0] * heads
    key_dim, value_dim = keys.shape[1] // heads, values.shape[1] // heads
    state = pltpu.VMEM((CHUNKS, key_dim, value_dim // CHUNKS), BF16)
    total = pltpu.VMEM((CHUNKS, key_dim, value_dim // CHUNKS), F32)
    dma = pltpu.SemaphoreType.DMA
    hbm, vmem = pl.BlockSpec(memory_space=pltpu.HBM), pl.BlockSpec(memory_space=pltpu.VMEM)
    wides = (value_dim, key_dim, key_dim, value_dim)
    outs = [jax.ShapeDtypeStruct((tokens, width), BF16) for width in wides]
    lengths = doc_lengths.reshape(1, -1)
    results = pl.pallas_call(
        functools.partial(kernel, shards, heads),
        out_shape=[pltpu.VMEM((tokens, width), BF16) for width in wides],
        in_specs=[hbm] * 6,
        out_specs=[vmem] * 4,
        scratch_shapes=[
            pltpu.VMEM((tokens, width), BF16) for width in (key_dim, key_dim, value_dim, value_dim)
        ]
        + [pltpu.VMEM(log_decay.shape, F32), pltpu.VMEM(lengths.shape, jnp.int32)]
        + [total] * 2
        + [state] * 8
        + [pltpu.VMEM((tokens, width), F32) for width in wides]
        + [dma((2 + PARTS, heads - 1)), dma((2 + PARTS, heads - 1)), dma((5 + PARTS,))]
        + [dma((CHUNKS,))] * 8,
        compiler_params=pltpu.CompilerParams(
            collective_id=0, has_side_effects=True, vmem_limit_bytes=40 * 1024 * 1024
        ),
    )(*[
        pltpu.with_memory_space_constraint(x, pltpu.HBM)
        for x in (queries, keys, values, grad_out, log_decay, lengths)
    ])
    return tuple(pl.pallas_call(
        leave,
        out_shape=outs,
        in_specs=[vmem] * 4,
        out_specs=[hbm] * 4,
        scratch_shapes=[dma((4,))],
    )(*results))


def solution(mesh):
    shards, heads = mesh.shape["ctx"], mesh.shape["head"]

    def whole(queries, keys, values, grad_out, log_decay, doc_lengths):
        window = queries.shape[0]
        tokens = window // shards
        reach = -(-(window // 4 - 1) // tokens)
        short = reach <= 2 and shards % 2 == 0 and tokens == BLOCK and (tokens // heads) % 16 == 0
        placed = (
            P(("ctx", "head"), None),
            P(("ctx", "head"), None),
            P(("ctx", "head"), None),
            P("ctx", "head"),
            P("head", "ctx"),
            P(),
        )
        return jax.shard_map(
            paired if short else per_device,
            mesh=mesh,
            in_specs=placed,
            out_specs=(P("ctx", "head"), P("ctx", "head"), P("ctx", "head"), P("ctx", "head")),
            check_vma=False,
        )(queries, keys, values, grad_out, log_decay, doc_lengths)

    return whole
```

```python
import jax
import jax.numpy as jnp
import functools

from jax import lax
from jax.experimental import pallas as pl
from jax.experimental.pallas import tpu as pltpu
from jax.sharding import PartitionSpec as P

BLOCK = 128


def passed_along(block, axis, distance):
    devices = range(lax.axis_size(axis))
    route = [(i - distance, i) for i in devices if i - distance in devices]
    return lax.ppermute(block, axis, route)


def document_ids(doc_lengths, first_place, span_length):
    starts = jnp.cumsum(doc_lengths, dtype=jnp.int32) - doc_lengths
    places = first_place - 1 + jnp.arange(span_length + 1, dtype=jnp.int32)
    return jnp.sum((starts[None, :] <= places[:, None]).astype(jnp.int32), axis=1) - 1


def decay_tables(log_rates, doc_ids, block_size, score_scaling):
    block_count = log_rates.shape[0] // block_size
    cumulated = jnp.cumsum(log_rates.reshape(block_count, block_size), axis=1)
    before = doc_ids[0 : block_count * block_size : block_size]
    own_ids = doc_ids[1:].reshape(block_count, block_size)
    carried = (own_ids == before[:, None]).astype(jnp.float32)
    last_ids = own_ids[:, block_size - 1]
    tail_mask = (own_ids == last_ids[:, None]).astype(jnp.float32)
    block_decay = jnp.exp(cumulated[:, block_size - 1]) * carried[:, block_size - 1]
    row_index = lax.broadcasted_iota(jnp.int32, (block_size, block_size), 0)
    column_index = lax.broadcasted_iota(jnp.int32, (block_size, block_size), 1)
    inside = (own_ids[:, :, None] == own_ids[:, None, :]) & (row_index >= column_index)[None]
    decay_gaps = cumulated[:, :, None] - cumulated[:, None, :]
    weights = jnp.where(inside, jnp.exp(jnp.where(inside, decay_gaps, 0.0)), 0.0) * score_scaling
    per_head_decay_rate = jnp.exp(cumulated) * carried
    tail_decay = jnp.exp(cumulated[:, block_size - 1 :] - cumulated) * tail_mask
    return (weights, per_head_decay_rate, tail_decay, block_decay)


def chain_combine(earlier, follower):
    return (earlier[0] * follower[0], follower[0] * earlier[1] + follower[1])


def offset_list(shard_total):
    return [1] + [1 << level for level in range((shard_total - 1).bit_length())]


def per_device(queries, keys, values, grad_out, log_decay, doc_lengths):
    query_rows, key_rows, value_rows = (
        lax.all_to_all(queries, "head", split_axis=1, concat_axis=0, tiled=True),
        lax.all_to_all(keys, "head", split_axis=1, concat_axis=0, tiled=True),
        lax.all_to_all(values, "head", split_axis=1, concat_axis=0, tiled=True),
    )
    tok_dev, key_dim = key_rows.shape
    value_dim = value_rows.shape[1]
    block_count = tok_dev // BLOCK
    score_scaling = (key_dim * BLOCK) ** (-0.5)
    shard_total = lax.axis_size("ctx")
    doc_ids = document_ids(doc_lengths, lax.axis_index("ctx") * tok_dev, tok_dev)
    weights, per_head_decay_rate, tail_decay, block_decay = decay_tables(
        log_decay[0], doc_ids, BLOCK, score_scaling
    )
    query_block_list = query_rows.reshape(block_count, BLOCK, key_dim)
    key_blocks = key_rows.reshape(block_count, BLOCK, key_dim)
    value_block_list = value_rows.reshape(block_count, BLOCK, value_dim)
    gradient_block_list = grad_out.reshape(block_count, BLOCK, value_dim)
    zero_state = jnp.zeros((key_dim, value_dim), jnp.float32)
    keyed_blocks = (key_blocks * tail_decay[:, :, None]).astype(jnp.bfloat16)
    updates = jnp.einsum(
        "ncd,nce->nde", keyed_blocks, value_block_list, preferred_element_type=jnp.float32
    )
    local_starts = []
    running = zero_state
    factor = jnp.float32(1.0)
    block_index = 0
    local_starts.append(running)
    carry_gains = factor
    running = block_decay[block_index] * running + updates[block_index]
    factor = factor * block_decay[block_index]
    shard_decay = factor
    current = (shard_decay, running)
    for position, offset in enumerate(offset_list(shard_total)):
        pulled = passed_along((current[0], current[1]), "ctx", offset)
        current = pulled if position == 0 else chain_combine(pulled, current)
    incoming = current[1]
    states = jnp.stack([carry_gains * incoming])
    queried = (query_block_list * (per_head_decay_rate * score_scaling)[:, :, None]).astype(
        jnp.bfloat16
    )
    back_updates = jnp.einsum(
        "ncd,nce->nde", queried, gradient_block_list, preferred_element_type=jnp.float32
    )
    local_ends = [zero_state] * block_count
    back_gains = [jnp.float32(1.0)] * block_count
    running = zero_state
    factor = jnp.float32(1.0)
    for block_index in reversed(range(block_count)):
        local_ends[block_index] = running
        back_gains[block_index] = factor
        running = block_decay[block_index] * running + back_updates[block_index]
        factor = factor * block_decay[block_index]
    current = (shard_decay, running)
    for position, offset in enumerate(offset_list(shard_total)):
        pulled = passed_along((current[0], current[1]), "ctx", -offset)
        current = pulled if position == 0 else chain_combine(pulled, current)
    arriving = current[1]
    ends = jnp.stack([back_gains[0] * arriving])
    lowered_state = states.astype(jnp.bfloat16)
    back_low = ends.astype(jnp.bfloat16)
    scores = jnp.einsum(
        "nid,njd->nij", query_block_list, key_blocks, preferred_element_type=jnp.float32
    )
    attention_weights = (scores * weights).astype(jnp.bfloat16)
    retained = (
        jnp.einsum(
            "xho,xoy->xhy", query_block_list, lowered_state, preferred_element_type=jnp.float32
        )
        * (per_head_decay_rate * score_scaling)[:, :, None]
    )
    retained = retained + jnp.einsum(
        "bcv,bvd->bcd", attention_weights, value_block_list, preferred_element_type=jnp.float32
    )
    score_gradient = jnp.einsum(
        "ysb,ytb->yst", gradient_block_list, value_block_list, preferred_element_type=jnp.float32
    )
    gprobs = (score_gradient * weights).astype(jnp.bfloat16)
    query_gradient = (
        jnp.einsum(
            "srj,sqj->srq", gradient_block_list, lowered_state, preferred_element_type=jnp.float32
        )
        * (per_head_decay_rate * score_scaling)[:, :, None]
    )
    query_gradient = query_gradient + jnp.einsum(
        "nij,njd->nid", gprobs, key_blocks, preferred_element_type=jnp.float32
    )
    grad_k = (
        jnp.einsum("nje,nde->njd", value_block_list, back_low, preferred_element_type=jnp.float32)
        * tail_decay[:, :, None]
    )
    grad_k = grad_k + jnp.einsum(
        "nij,nid->njd", gprobs, query_block_list, preferred_element_type=jnp.float32
    )
    value_gradient = (
        jnp.einsum("njd,nde->nje", key_blocks, back_low, preferred_element_type=jnp.float32)
        * tail_decay[:, :, None]
    )
    value_gradient = value_gradient + jnp.einsum(
        "glu,glx->gux", attention_weights, gradient_block_list, preferred_element_type=jnp.float32
    )
    return (
        retained.reshape(tok_dev, value_dim).astype(jnp.bfloat16),
        query_gradient.reshape(tok_dev, key_dim).astype(jnp.bfloat16),
        grad_k.reshape(tok_dev, key_dim).astype(jnp.bfloat16),
        value_gradient.reshape(tok_dev, value_dim).astype(jnp.bfloat16),
    )


CHUNKS = 4
PARTS = 2
MESH = pl.DeviceIdType.MESH
F32, BF16 = jnp.float32, jnp.bfloat16


def dot(left, right, left_dim, right_dim):
    return lax.dot_general(
        left, right, (((left_dim,), (right_dim,)), ((), ())), preferred_element_type=F32
    )


def kernel(
    shards,
    heads,
    q_ref, k_ref, v_ref, g_ref, log_hbm, len_hbm,
    ret_ref, dq_ref, dk_ref, dv_ref,
    q_all, k_all, v_all, g_all, log_ref, len_ref,
    u_buf, w_buf,
    f_first_out, f_first_in, f_state_out, f_state_in,
    b_first_out, b_first_in, b_state_out, b_state_in,
    ret_part, dq_part, dk_part, dv_part,
    head_send, head_recv, local_sem,
    f_first_send, f_first_recv, f_state_send, f_state_recv,
    b_first_send, b_first_recv, b_state_send, b_state_recv,
):
    c, h = lax.axis_index("ctx"), lax.axis_index("head")
    rows = q_ref.shape[0]
    tokens, key_dim = q_all.shape
    value_dim = v_all.shape[1]
    width = value_dim // CHUNKS
    part = value_dim // PARTS
    scale = (key_dim * BLOCK) ** -0.5
    even = lax.rem(c, 2) == 0
    odd = jnp.logical_not(even)
    has_earlier, has_later = c > 0, c < shards - 1

    def columns(n):
        return slice(n * width, (n + 1) * width)

    barrier = pltpu.get_barrier_semaphore()
    for offset in range(1, heads):
        pl.semaphore_signal(
            barrier, inc=1, device_id=(c, lax.rem(h + offset, heads)), device_id_type=MESH
        )

    @pl.when(has_earlier)
    def _():
        pl.semaphore_signal(barrier, inc=1, device_id=(c - 1, h), device_id_type=MESH)

    @pl.when(has_later)
    def _():
        pl.semaphore_signal(barrier, inc=1, device_id=(c + 1, h), device_id_type=MESH)

    def head_copy(number, target_head, place_head):
        if number < 2:
            source, gathered = ((q_ref, q_all), (k_ref, k_all))[number]
            span, place = key_dim, pl.ds(0, key_dim)
            begin = target_head * key_dim
        else:
            source, gathered, span = v_ref, v_all, part
            place = pl.ds((number - 2) * part, part)
            begin = target_head * value_dim + (number - 2) * part
        held = pl.ds(pl.multiple_of(place_head * rows, rows), rows)
        return source.at[:, pl.ds(pl.multiple_of(begin, span), span)], gathered.at[held, place]

    pieces = 2 + PARTS
    own = [
        pltpu.make_async_copy(*head_copy(number, h, h), local_sem.at[number])
        for number in range(pieces)
    ]
    small = [
        pltpu.make_async_copy(log_hbm, log_ref, local_sem.at[pieces]),
        pltpu.make_async_copy(len_hbm, len_ref, local_sem.at[pieces + 1]),
    ]
    own_g = pltpu.make_async_copy(g_ref, g_all, local_sem.at[pieces + 2])
    for copy in small + own[:1] + [own_g] + own[1:]:
        copy.start()

    pl.semaphore_wait(
        barrier, heads - 1 + has_earlier.astype(jnp.int32) + has_later.astype(jnp.int32)
    )

    def exchanged(number, offset, incoming):
        peer = lax.rem(h + (heads - offset if incoming else offset), heads)
        source, target = head_copy(number, peer, peer if incoming else h)
        return pltpu.make_async_remote_copy(
            src_ref=source, dst_ref=target,
            send_sem=head_send.at[number, offset - 1], recv_sem=head_recv.at[number, offset - 1],
            device_id=(c, peer), device_id_type=MESH,
        )

    for offset in range(1, heads):
        exchanged(0, offset, False).start()

    def arrived(number):
        own[number].wait()
        for offset in range(1, heads):
            exchanged(number, offset, True).wait_recv()

    for copy in small:
        copy.wait()
    i = lax.broadcasted_iota(jnp.int32, (tokens, tokens), 0)
    j = lax.broadcasted_iota(jnp.int32, (tokens, tokens), 1)
    cum_col = jnp.sum(jnp.where(j <= i, log_ref[...], 0.0), axis=1, keepdims=True)
    cum_row = jnp.sum(jnp.where(i == j, cum_col, 0.0), axis=0, keepdims=True)
    documents = len_ref.shape[1]
    d = lax.broadcasted_iota(jnp.int32, (documents, documents), 0)
    e = lax.broadcasted_iota(jnp.int32, (documents, documents), 1)
    lengths = len_ref[...].astype(F32)
    starts = jnp.sum(jnp.where(e < d, lengths, 0.0), axis=1, keepdims=True)
    first = c * tokens
    places = (lax.broadcasted_iota(jnp.int32, (documents, tokens), 1) + first).astype(F32)
    doc_row = jnp.sum(jnp.where(starts <= places, 1.0, 0.0), axis=0, keepdims=True)
    before_place = (lax.broadcasted_iota(jnp.int32, (documents, 1), 1) + (first - 1)).astype(F32)
    doc_before = jnp.sum(jnp.where(starts <= before_place, 1.0, 0.0), axis=0, keepdims=True)
    doc_col = jnp.sum(jnp.where(i == j, doc_row, 0.0), axis=1, keepdims=True)
    last_lane = lax.broadcasted_iota(jnp.int32, (1, tokens), 1) == tokens - 1
    doc_last = jnp.sum(jnp.where(last_lane, doc_row, 0.0), axis=1, keepdims=True)
    cum_last = jnp.sum(jnp.where(last_lane, cum_row, 0.0), axis=1, keepdims=True)
    inside = (doc_col == doc_row) & (j <= i)
    weights = jnp.where(inside, jnp.exp(jnp.where(inside, cum_col - cum_row, 0.0)), 0.0) * scale
    rate = jnp.where(doc_col == doc_before, jnp.exp(cum_col), 0.0) * scale
    tail = jnp.where(doc_col == doc_last, jnp.exp(cum_last - cum_col), 0.0)
    decay = jnp.where(doc_last == doc_before, jnp.exp(cum_last), 0.0)

    for number in range(1, pieces - 1):
        for offset in range(1, heads):
            exchanged(number, offset, False).start()

    def passing(update, first_out, first_in, state_out, state_in,
                first_send, first_recv, state_send, state_recv, opens, target, has_source, has_target):
        closes = jnp.logical_not(opens)

        def first_copy(n):
            return pltpu.make_async_remote_copy(
                src_ref=first_out.at[n], dst_ref=first_in.at[n],
                send_sem=first_send.at[n], recv_sem=first_recv.at[n],
                device_id=(target, h), device_id_type=MESH,
            )

        def state_copy(n):
            return pltpu.make_async_remote_copy(
                src_ref=state_out.at[n], dst_ref=state_in.at[n],
                send_sem=state_send.at[n], recv_sem=state_recv.at[n],
                device_id=(target, h), device_id_type=MESH,
            )

        def open_pair(n):
            @pl.when(opens)
            def _():
                first_out[n] = update[n].astype(BF16)
                first_copy(n).start()

        def close_pair():
            @pl.when(closes)
            def _():
                for n in range(CHUNKS):
                    close_chunk(n)

        def close_chunk(n):
            first_copy(n).wait_recv()

            @pl.when(has_target)
            def _():
                state_out[n] = (update[n] + decay * first_in[n].astype(F32)).astype(BF16)
                state_copy(n).start()

        def relay(n):
            @pl.when(has_source)
            def _():
                state_copy(n).wait_recv()

            @pl.when(jnp.logical_not(has_source))
            def _():
                state_in[n] = jnp.zeros(state_in.shape[1:], BF16)

            @pl.when(opens)
            def _():
                state_out[n] = (update[n] + decay * state_in[n].astype(F32)).astype(BF16)
                state_copy(n).start()

        def finish():
            @pl.when(opens)
            def _():
                for n in range(CHUNKS):
                    first_copy(n).wait_send()

            @pl.when(has_target)
            def _():
                for n in range(CHUNKS):
                    state_copy(n).wait_send()

        return open_pair, close_pair, close_chunk, relay, finish

    f_open, _, f_close_chunk, f_relay, f_finish = passing(
        u_buf, f_first_out, f_first_in, f_state_out, f_state_in,
        f_first_send, f_first_recv, f_state_send, f_state_recv,
        even, c + 1, has_earlier, has_later,
    )
    b_open, b_close, _, b_relay, b_finish = passing(
        w_buf, b_first_out, b_first_in, b_state_out, b_state_in,
        b_first_send, b_first_recv, b_state_send, b_state_recv,
        odd, c - 1, has_later, has_earlier,
    )

    per_part = CHUNKS // PARTS

    def halves(n):
        return slice(n * part, (n + 1) * part)

    own_g.wait()
    arrived(0)
    queried = (q_all[...].astype(F32) * rate).T.astype(BF16)
    for m in range(PARTS):
        product = dot(queried, g_all[:, halves(m)], 1, 0)
        for n in range(per_part):
            w_buf[m * per_part + n] = product[:, columns(n)]
            b_open(m * per_part + n)
    for offset in range(1, heads):
        exchanged(pieces - 1, offset, False).start()
    b_close()

    arrived(1)
    keyed = (k_all[...].astype(F32) * tail).T.astype(BF16)
    probs = (dot(q_all[...], k_all[...], 1, 1) * weights).astype(BF16)
    for m in range(PARTS):
        arrived(2 + m)
        product = dot(keyed, v_all[:, halves(m)], 1, 0)
        for n in range(per_part):
            u_buf[m * per_part + n] = product[:, columns(n)]
            f_open(m * per_part + n)
        if m == 0:
            dv_part[...] = dot(probs, g_all[...], 0, 0)

        @pl.when(odd)
        def _():
            for n in range(per_part):
                f_close_chunk(m * per_part + n)

    gprobs = (dot(g_all[...], v_all[...], 1, 1) * weights).astype(BF16)
    dk_part[...] = dot(gprobs, q_all[...], 0, 0)
    dq_part[...] = dot(gprobs, k_all[...], 1, 0)
    ret_part[...] = dot(probs, v_all[...], 1, 0)

    def joined(relay, state_in, m):
        chunks = range(m * per_part, (m + 1) * per_part)
        for n in chunks:
            relay(n)
        return jnp.concatenate([state_in[n] for n in chunks], axis=1)

    total = jnp.zeros((tokens, key_dim), F32)
    for m in range(PARTS):
        back = joined(b_relay, b_state_in, m)
        dv_ref[:, halves(m)] = (
            dot(k_all[...], back, 1, 0) * tail + dv_part[:, halves(m)]
        ).astype(BF16)
        total += dot(v_all[:, halves(m)], back, 1, 1)
    dk_ref[...] = (total * tail + dk_part[...]).astype(BF16)

    total = jnp.zeros((tokens, key_dim), F32)
    for m in range(PARTS):
        state = joined(f_relay, f_state_in, m)
        ret_ref[:, halves(m)] = (
            dot(q_all[...], state, 1, 0) * rate + ret_part[:, halves(m)]
        ).astype(BF16)
        total += dot(g_all[:, halves(m)], state, 1, 1)
    dq_ref[...] = (total * rate + dq_part[...]).astype(BF16)

    for number in range(pieces):
        for offset in range(1, heads):
            exchanged(number, offset, False).wait_send()
    b_finish()
    f_finish()


def leave(*refs):
    count = len(refs) // 2
    sem = refs[-1]
    copies = [
        pltpu.make_async_copy(refs[n], refs[count + n], sem.at[n]) for n in range(count)
    ]
    for copy in copies:
        copy.start()
    for copy in copies:
        copy.wait()


def paired(queries, keys, values, grad_out, log_decay, doc_lengths):
    shards, heads = lax.axis_size("ctx"), lax.axis_size("head")
    tokens = queries.shape[0] * heads
    key_dim, value_dim = keys.shape[1] // heads, values.shape[1] // heads
    state = pltpu.VMEM((CHUNKS, key_dim, value_dim // CHUNKS), BF16)
    total = pltpu.VMEM((CHUNKS, key_dim, value_dim // CHUNKS), F32)
    dma = pltpu.SemaphoreType.DMA
    hbm, vmem = pl.BlockSpec(memory_space=pltpu.HBM), pl.BlockSpec(memory_space=pltpu.VMEM)
    wides = (value_dim, key_dim, key_dim, value_dim)
    outs = [jax.ShapeDtypeStruct((tokens, width), BF16) for width in wides]
    lengths = doc_lengths.reshape(1, -1)
    results = pl.pallas_call(
        functools.partial(kernel, shards, heads),
        out_shape=[pltpu.VMEM((tokens, width), BF16) for width in wides],
        in_specs=[hbm] * 6,
        out_specs=[vmem] * 4,
        scratch_shapes=[
            pltpu.VMEM((tokens, width), BF16) for width in (key_dim, key_dim, value_dim, value_dim)
        ]
        + [pltpu.VMEM(log_decay.shape, F32), pltpu.VMEM(lengths.shape, jnp.int32)]
        + [total] * 2
        + [state] * 8
        + [pltpu.VMEM((tokens, width), F32) for width in wides]
        + [dma((2 + PARTS, heads - 1)), dma((2 + PARTS, heads - 1)), dma((5 + PARTS,))]
        + [dma((CHUNKS,))] * 8,
        compiler_params=pltpu.CompilerParams(
            collective_id=0, has_side_effects=True, vmem_limit_bytes=40 * 1024 * 1024
        ),
    )(*[
        pltpu.with_memory_space_constraint(x, pltpu.HBM)
        for x in (queries, keys, values, grad_out, log_decay, lengths)
    ])
    return tuple(pl.pallas_call(
        leave,
        out_shape=outs,
        in_specs=[vmem] * 4,
        out_specs=[hbm] * 4,
        scratch_shapes=[dma((4,))],
        compiler_params=pltpu.CompilerParams(vmem_limit_bytes=1024 * 1024),
    )(*results))


def solution(mesh):
    shards, heads = mesh.shape["ctx"], mesh.shape["head"]

    def whole(queries, keys, values, grad_out, log_decay, doc_lengths):
        window = queries.shape[0]
        tokens = window // shards
        reach = -(-(window // 4 - 1) // tokens)
        short = reach <= 2 and shards % 2 == 0 and tokens == BLOCK and (tokens // heads) % 16 == 0
        placed = (
            P(("ctx", "head"), None),
            P(("ctx", "head"), None),
            P(("ctx", "head"), None),
            P("ctx", "head"),
            P("head", "ctx"),
            P(),
        )
        return jax.shard_map(
            paired if short else per_device,
            mesh=mesh,
            in_specs=placed,
            out_specs=(P("ctx", "head"), P("ctx", "head"), P("ctx", "head"), P("ctx", "head")),
            check_vma=False,
        )(queries, keys, values, grad_out, log_decay, doc_lengths)

    return whole
```

```python
import jax
import jax.numpy as jnp
import functools

from jax import lax
from jax.experimental import pallas as pl
from jax.experimental.pallas import tpu as pltpu
from jax.sharding import PartitionSpec as P

BLOCK = 128


def passed_along(block, axis, distance):
    devices = range(lax.axis_size(axis))
    route = [(i - distance, i) for i in devices if i - distance in devices]
    return lax.ppermute(block, axis, route)


def document_ids(doc_lengths, first_place, span_length):
    starts = jnp.cumsum(doc_lengths, dtype=jnp.int32) - doc_lengths
    places = first_place - 1 + jnp.arange(span_length + 1, dtype=jnp.int32)
    return jnp.sum((starts[None, :] <= places[:, None]).astype(jnp.int32), axis=1) - 1


def decay_tables(log_rates, doc_ids, block_size, score_scaling):
    block_count = log_rates.shape[0] // block_size
    cumulated = jnp.cumsum(log_rates.reshape(block_count, block_size), axis=1)
    before = doc_ids[0 : block_count * block_size : block_size]
    own_ids = doc_ids[1:].reshape(block_count, block_size)
    carried = (own_ids == before[:, None]).astype(jnp.float32)
    last_ids = own_ids[:, block_size - 1]
    tail_mask = (own_ids == last_ids[:, None]).astype(jnp.float32)
    block_decay = jnp.exp(cumulated[:, block_size - 1]) * carried[:, block_size - 1]
    row_index = lax.broadcasted_iota(jnp.int32, (block_size, block_size), 0)
    column_index = lax.broadcasted_iota(jnp.int32, (block_size, block_size), 1)
    inside = (own_ids[:, :, None] == own_ids[:, None, :]) & (row_index >= column_index)[None]
    decay_gaps = cumulated[:, :, None] - cumulated[:, None, :]
    weights = jnp.where(inside, jnp.exp(jnp.where(inside, decay_gaps, 0.0)), 0.0) * score_scaling
    per_head_decay_rate = jnp.exp(cumulated) * carried
    tail_decay = jnp.exp(cumulated[:, block_size - 1 :] - cumulated) * tail_mask
    return (weights, per_head_decay_rate, tail_decay, block_decay)


def chain_combine(earlier, follower):
    return (earlier[0] * follower[0], follower[0] * earlier[1] + follower[1])


def offset_list(shard_total):
    return [1] + [1 << level for level in range((shard_total - 1).bit_length())]


def per_device(queries, keys, values, grad_out, log_decay, doc_lengths):
    query_rows, key_rows, value_rows = (
        lax.all_to_all(queries, "head", split_axis=1, concat_axis=0, tiled=True),
        lax.all_to_all(keys, "head", split_axis=1, concat_axis=0, tiled=True),
        lax.all_to_all(values, "head", split_axis=1, concat_axis=0, tiled=True),
    )
    tok_dev, key_dim = key_rows.shape
    value_dim = value_rows.shape[1]
    block_count = tok_dev // BLOCK
    score_scaling = (key_dim * BLOCK) ** (-0.5)
    shard_total = lax.axis_size("ctx")
    doc_ids = document_ids(doc_lengths, lax.axis_index("ctx") * tok_dev, tok_dev)
    weights, per_head_decay_rate, tail_decay, block_decay = decay_tables(
        log_decay[0], doc_ids, BLOCK, score_scaling
    )
    query_block_list = query_rows.reshape(block_count, BLOCK, key_dim)
    key_blocks = key_rows.reshape(block_count, BLOCK, key_dim)
    value_block_list = value_rows.reshape(block_count, BLOCK, value_dim)
    gradient_block_list = grad_out.reshape(block_count, BLOCK, value_dim)
    zero_state = jnp.zeros((key_dim, value_dim), jnp.float32)
    keyed_blocks = (key_blocks * tail_decay[:, :, None]).astype(jnp.bfloat16)
    updates = jnp.einsum(
        "ncd,nce->nde", keyed_blocks, value_block_list, preferred_element_type=jnp.float32
    )
    local_starts = []
    running = zero_state
    factor = jnp.float32(1.0)
    block_index = 0
    local_starts.append(running)
    carry_gains = factor
    running = block_decay[block_index] * running + updates[block_index]
    factor = factor * block_decay[block_index]
    shard_decay = factor
    current = (shard_decay, running)
    for position, offset in enumerate(offset_list(shard_total)):
        pulled = passed_along((current[0], current[1]), "ctx", offset)
        current = pulled if position == 0 else chain_combine(pulled, current)
    incoming = current[1]
    states = jnp.stack([carry_gains * incoming])
    queried = (query_block_list * (per_head_decay_rate * score_scaling)[:, :, None]).astype(
        jnp.bfloat16
    )
    back_updates = jnp.einsum(
        "ncd,nce->nde", queried, gradient_block_list, preferred_element_type=jnp.float32
    )
    local_ends = [zero_state] * block_count
    back_gains = [jnp.float32(1.0)] * block_count
    running = zero_state
    factor = jnp.float32(1.0)
    for block_index in reversed(range(block_count)):
        local_ends[block_index] = running
        back_gains[block_index] = factor
        running = block_decay[block_index] * running + back_updates[block_index]
        factor = factor * block_decay[block_index]
    current = (shard_decay, running)
    for position, offset in enumerate(offset_list(shard_total)):
        pulled = passed_along((current[0], current[1]), "ctx", -offset)
        current = pulled if position == 0 else chain_combine(pulled, current)
    arriving = current[1]
    ends = jnp.stack([back_gains[0] * arriving])
    lowered_state = states.astype(jnp.bfloat16)
    back_low = ends.astype(jnp.bfloat16)
    scores = jnp.einsum(
        "nid,njd->nij", query_block_list, key_blocks, preferred_element_type=jnp.float32
    )
    attention_weights = (scores * weights).astype(jnp.bfloat16)
    retained = (
        jnp.einsum(
            "xho,xoy->xhy", query_block_list, lowered_state, preferred_element_type=jnp.float32
        )
        * (per_head_decay_rate * score_scaling)[:, :, None]
    )
    retained = retained + jnp.einsum(
        "bcv,bvd->bcd", attention_weights, value_block_list, preferred_element_type=jnp.float32
    )
    score_gradient = jnp.einsum(
        "ysb,ytb->yst", gradient_block_list, value_block_list, preferred_element_type=jnp.float32
    )
    gprobs = (score_gradient * weights).astype(jnp.bfloat16)
    query_gradient = (
        jnp.einsum(
            "srj,sqj->srq", gradient_block_list, lowered_state, preferred_element_type=jnp.float32
        )
        * (per_head_decay_rate * score_scaling)[:, :, None]
    )
    query_gradient = query_gradient + jnp.einsum(
        "nij,njd->nid", gprobs, key_blocks, preferred_element_type=jnp.float32
    )
    grad_k = (
        jnp.einsum("nje,nde->njd", value_block_list, back_low, preferred_element_type=jnp.float32)
        * tail_decay[:, :, None]
    )
    grad_k = grad_k + jnp.einsum(
        "nij,nid->njd", gprobs, query_block_list, preferred_element_type=jnp.float32
    )
    value_gradient = (
        jnp.einsum("njd,nde->nje", key_blocks, back_low, preferred_element_type=jnp.float32)
        * tail_decay[:, :, None]
    )
    value_gradient = value_gradient + jnp.einsum(
        "glu,glx->gux", attention_weights, gradient_block_list, preferred_element_type=jnp.float32
    )
    return (
        retained.reshape(tok_dev, value_dim).astype(jnp.bfloat16),
        query_gradient.reshape(tok_dev, key_dim).astype(jnp.bfloat16),
        grad_k.reshape(tok_dev, key_dim).astype(jnp.bfloat16),
        value_gradient.reshape(tok_dev, value_dim).astype(jnp.bfloat16),
    )


CHUNKS = 4
PARTS = 2
HEADS = 4
MESH = pl.DeviceIdType.MESH
F32, BF16 = jnp.float32, jnp.bfloat16


def dot(left, right, left_dim, right_dim):
    return lax.dot_general(
        left, right, (((left_dim,), (right_dim,)), ((), ())), preferred_element_type=F32
    )


def kernel(
    shards,
    heads,
    q_ref, k_ref, v_ref, g_ref, log_hbm, len_hbm,
    ret_ref, dq_ref, dk_ref, dv_ref,
    q_all, k_all, v_all, g_all, log_ref, len_ref,
    u_buf, w_buf,
    f_first_out, f_first_in, f_state_out, f_state_in,
    b_first_out, b_first_in, b_state_out, b_state_in,
    ret_part, dq_part, dk_part, dv_part,
    head_send, head_recv, local_sem,
    f_first_send, f_first_recv, f_state_send, f_state_recv,
    b_first_send, b_first_recv, b_state_send, b_state_recv,
):
    c, h = lax.axis_index("ctx"), lax.axis_index("head")
    rows = q_ref.shape[0]
    tokens, key_dim = q_all.shape
    value_dim = v_all.shape[1]
    width = value_dim // CHUNKS
    part = value_dim // PARTS
    scale = (key_dim * BLOCK) ** -0.5
    even = lax.rem(c, 2) == 0
    odd = jnp.logical_not(even)
    has_earlier, has_later = c > 0, c < shards - 1

    def columns(n):
        return slice(n * width, (n + 1) * width)

    barrier = pltpu.get_barrier_semaphore()
    for offset in range(1, heads):
        pl.semaphore_signal(
            barrier, inc=1, device_id=(c, lax.rem(h + offset, heads)), device_id_type=MESH
        )

    @pl.when(has_earlier)
    def _():
        pl.semaphore_signal(barrier, inc=1, device_id=(c - 1, h), device_id_type=MESH)

    @pl.when(has_later)
    def _():
        pl.semaphore_signal(barrier, inc=1, device_id=(c + 1, h), device_id_type=MESH)

    partners = (HEADS - 1 - h, lax.rem(h + 2, HEADS), h + 1 - 2 * lax.rem(h, 2))

    def head_copy(number, target_head, place_head):
        source, gathered = ((q_ref, q_all), (k_ref, k_all), (v_ref, v_all))[number]
        span = gathered.shape[1]
        begin = target_head * span
        held = pl.ds(pl.multiple_of(place_head * rows, rows), rows)
        return source.at[:, pl.ds(pl.multiple_of(begin, span), span)], gathered.at[held]

    pieces = 3
    own = [
        pltpu.make_async_copy(*head_copy(number, h, h), local_sem.at[number])
        for number in range(pieces)
    ]
    small = [
        pltpu.make_async_copy(log_hbm, log_ref, local_sem.at[pieces]),
        pltpu.make_async_copy(len_hbm, len_ref, local_sem.at[pieces + 1]),
    ]
    own_g = pltpu.make_async_copy(g_ref, g_all, local_sem.at[pieces + 2])
    for copy in small + own[:1] + [own_g] + own[1:]:
        copy.start()

    pl.semaphore_wait(
        barrier, heads - 1 + has_earlier.astype(jnp.int32) + has_later.astype(jnp.int32)
    )

    def exchanged(number, p, incoming):
        peer = partners[p]
        source, target = head_copy(number, peer, peer if incoming else h)
        return pltpu.make_async_remote_copy(
            src_ref=source, dst_ref=target,
            send_sem=head_send.at[number, p], recv_sem=head_recv.at[number, p],
            device_id=(c, peer), device_id_type=MESH,
        )

    for number in range(pieces):
        for p in range(len(partners)):
            exchanged(number, p, False).start()

    def arrived(number):
        own[number].wait()
        for p in range(len(partners)):
            exchanged(number, p, True).wait_recv()

    for copy in small:
        copy.wait()
    i = lax.broadcasted_iota(jnp.int32, (tokens, tokens), 0)
    j = lax.broadcasted_iota(jnp.int32, (tokens, tokens), 1)
    cum_col = jnp.sum(jnp.where(j <= i, log_ref[...], 0.0), axis=1, keepdims=True)
    cum_row = jnp.sum(jnp.where(i == j, cum_col, 0.0), axis=0, keepdims=True)
    documents = len_ref.shape[1]
    d = lax.broadcasted_iota(jnp.int32, (documents, documents), 0)
    e = lax.broadcasted_iota(jnp.int32, (documents, documents), 1)
    lengths = len_ref[...].astype(F32)
    starts = jnp.sum(jnp.where(e < d, lengths, 0.0), axis=1, keepdims=True)
    first = c * tokens
    places = (lax.broadcasted_iota(jnp.int32, (documents, tokens), 1) + first).astype(F32)
    doc_row = jnp.sum(jnp.where(starts <= places, 1.0, 0.0), axis=0, keepdims=True)
    before_place = (lax.broadcasted_iota(jnp.int32, (documents, 1), 1) + (first - 1)).astype(F32)
    doc_before = jnp.sum(jnp.where(starts <= before_place, 1.0, 0.0), axis=0, keepdims=True)
    doc_col = jnp.sum(jnp.where(i == j, doc_row, 0.0), axis=1, keepdims=True)
    last_lane = lax.broadcasted_iota(jnp.int32, (1, tokens), 1) == tokens - 1
    doc_last = jnp.sum(jnp.where(last_lane, doc_row, 0.0), axis=1, keepdims=True)
    cum_last = jnp.sum(jnp.where(last_lane, cum_row, 0.0), axis=1, keepdims=True)
    inside = (doc_col == doc_row) & (j <= i)
    weights = jnp.where(inside, jnp.exp(jnp.where(inside, cum_col - cum_row, 0.0)), 0.0) * scale
    rate = jnp.where(doc_col == doc_before, jnp.exp(cum_col), 0.0) * scale
    tail = jnp.where(doc_col == doc_last, jnp.exp(cum_last - cum_col), 0.0)
    decay = jnp.where(doc_last == doc_before, jnp.exp(cum_last), 0.0)

    def passing(update, first_out, first_in, state_out, state_in,
                first_send, first_recv, state_send, state_recv, opens, target, has_source, has_target):
        closes = jnp.logical_not(opens)

        def first_copy(n):
            return pltpu.make_async_remote_copy(
                src_ref=first_out.at[n], dst_ref=first_in.at[n],
                send_sem=first_send.at[n], recv_sem=first_recv.at[n],
                device_id=(target, h), device_id_type=MESH,
            )

        def state_copy(n):
            return pltpu.make_async_remote_copy(
                src_ref=state_out.at[n], dst_ref=state_in.at[n],
                send_sem=state_send.at[n], recv_sem=state_recv.at[n],
                device_id=(target, h), device_id_type=MESH,
            )

        def open_pair(n):
            @pl.when(opens)
            def _():
                first_out[n] = update[n].astype(BF16)
                first_copy(n).start()

        def close_pair():
            @pl.when(closes)
            def _():
                for n in range(CHUNKS):
                    close_chunk(n)

        def close_chunk(n):
            first_copy(n).wait_recv()

            @pl.when(has_target)
            def _():
                state_out[n] = (update[n] + decay * first_in[n].astype(F32)).astype(BF16)
                state_copy(n).start()

        def relay(n):
            @pl.when(has_source)
            def _():
                state_copy(n).wait_recv()

            @pl.when(jnp.logical_not(has_source))
            def _():
                state_in[n] = jnp.zeros(state_in.shape[1:], BF16)

            @pl.when(opens)
            def _():
                state_out[n] = (update[n] + decay * state_in[n].astype(F32)).astype(BF16)
                state_copy(n).start()

        def finish():
            @pl.when(opens)
            def _():
                for n in range(CHUNKS):
                    first_copy(n).wait_send()

            @pl.when(has_target)
            def _():
                for n in range(CHUNKS):
                    state_copy(n).wait_send()

        return open_pair, close_pair, relay, finish

    f_open, f_close, f_relay, f_finish = passing(
        u_buf, f_first_out, f_first_in, f_state_out, f_state_in,
        f_first_send, f_first_recv, f_state_send, f_state_recv,
        even, c + 1, has_earlier, has_later,
    )
    b_open, b_close, b_relay, b_finish = passing(
        w_buf, b_first_out, b_first_in, b_state_out, b_state_in,
        b_first_send, b_first_recv, b_state_send, b_state_recv,
        odd, c - 1, has_later, has_earlier,
    )

    per_part = CHUNKS // PARTS

    def halves(n):
        return slice(n * part, (n + 1) * part)

    own_g.wait()
    arrived(0)
    queried = (q_all[...].astype(F32) * rate).T.astype(BF16)
    product = dot(queried, g_all[...], 1, 0)
    for n in range(CHUNKS):
        w_buf[n] = product[:, columns(n)]
        b_open(n)

    arrived(1)
    keyed = (k_all[...].astype(F32) * tail).T.astype(BF16)
    arrived(2)
    product = dot(keyed, v_all[...], 1, 0)
    for n in range(CHUNKS):
        u_buf[n] = product[:, columns(n)]
        f_open(n)
    b_close()
    f_close()

    probs = (dot(q_all[...], k_all[...], 1, 1) * weights).astype(BF16)
    gprobs = (dot(g_all[...], v_all[...], 1, 1) * weights).astype(BF16)
    dv_part[...] = dot(probs, g_all[...], 0, 0)
    ret_part[...] = dot(probs, v_all[...], 1, 0)
    dk_part[...] = dot(gprobs, q_all[...], 0, 0)
    dq_part[...] = dot(gprobs, k_all[...], 1, 0)

    def directed(relay, state_in, left, right, factor, wide_part, narrow_part, wide_ref, narrow_ref, ahead):
        if ahead:
            for n in range(CHUNKS):
                relay(n)
        total = jnp.zeros((tokens, key_dim), F32)
        for m in range(PARTS):
            chunks = range(m * per_part, (m + 1) * per_part)
            if not ahead:
                for n in chunks:
                    relay(n)
            state = jnp.concatenate([state_in[n] for n in chunks], axis=1)
            wide_ref[:, halves(m)] = (
                dot(left[...], state, 1, 0) * factor + wide_part[:, halves(m)]
            ).astype(BF16)
            total += dot(right[:, halves(m)], state, 1, 1)
        narrow_ref[...] = (total * factor + narrow_part[...]).astype(BF16)

    forward = functools.partial(
        directed, f_relay, f_state_in, q_all, g_all, rate, ret_part, dq_part, ret_ref, dq_ref
    )
    backward = functools.partial(
        directed, b_relay, b_state_in, k_all, v_all, tail, dv_part, dk_part, dv_ref, dk_ref
    )

    @pl.when(even)
    def _():
        forward(True)
        backward(False)

    @pl.when(odd)
    def _():
        backward(True)
        forward(False)

    for number in range(pieces):
        for p in range(len(partners)):
            exchanged(number, p, False).wait_send()
    b_finish()
    f_finish()


def leave(*refs):
    count = len(refs) // 2
    sem = refs[-1]
    copies = [
        pltpu.make_async_copy(refs[n], refs[count + n], sem.at[n]) for n in range(count)
    ]
    for copy in copies:
        copy.start()
    for copy in copies:
        copy.wait()


def paired(queries, keys, values, grad_out, log_decay, doc_lengths):
    shards, heads = lax.axis_size("ctx"), lax.axis_size("head")
    tokens = queries.shape[0] * heads
    key_dim, value_dim = keys.shape[1] // heads, values.shape[1] // heads
    state = pltpu.VMEM((CHUNKS, key_dim, value_dim // CHUNKS), BF16)
    total = pltpu.VMEM((CHUNKS, key_dim, value_dim // CHUNKS), F32)
    dma = pltpu.SemaphoreType.DMA
    hbm, vmem = pl.BlockSpec(memory_space=pltpu.HBM), pl.BlockSpec(memory_space=pltpu.VMEM)
    wides = (value_dim, key_dim, key_dim, value_dim)
    outs = [jax.ShapeDtypeStruct((tokens, width), BF16) for width in wides]
    lengths = doc_lengths.reshape(1, -1)
    results = pl.pallas_call(
        functools.partial(kernel, shards, heads),
        out_shape=[pltpu.VMEM((tokens, width), BF16) for width in wides],
        in_specs=[hbm] * 6,
        out_specs=[vmem] * 4,
        scratch_shapes=[
            pltpu.VMEM((tokens, width), BF16) for width in (key_dim, key_dim, value_dim, value_dim)
        ]
        + [pltpu.VMEM(log_decay.shape, F32), pltpu.VMEM(lengths.shape, jnp.int32)]
        + [total] * 2
        + [state] * 8
        + [pltpu.VMEM((tokens, width), F32) for width in wides]
        + [dma((3, heads - 1)), dma((3, heads - 1)), dma((6,))]
        + [dma((CHUNKS,))] * 8,
        compiler_params=pltpu.CompilerParams(
            collective_id=0, has_side_effects=True, vmem_limit_bytes=40 * 1024 * 1024
        ),
    )(*[
        pltpu.with_memory_space_constraint(x, pltpu.HBM)
        for x in (queries, keys, values, grad_out, log_decay, lengths)
    ])
    return tuple(pl.pallas_call(
        leave,
        out_shape=outs,
        in_specs=[vmem] * 4,
        out_specs=[hbm] * 4,
        scratch_shapes=[dma((4,))],
        compiler_params=pltpu.CompilerParams(vmem_limit_bytes=1024 * 1024),
    )(*results))


def solution(mesh):
    shards, heads = mesh.shape["ctx"], mesh.shape["head"]

    def whole(queries, keys, values, grad_out, log_decay, doc_lengths):
        window = queries.shape[0]
        tokens = window // shards
        reach = -(-(window // 4 - 1) // tokens)
        short = reach <= 2 and shards % 2 == 0 and tokens == BLOCK and (tokens // heads) % 16 == 0
        short = short and heads == HEADS
        placed = (
            P(("ctx", "head"), None),
            P(("ctx", "head"), None),
            P(("ctx", "head"), None),
            P("ctx", "head"),
            P("head", "ctx"),
            P(),
        )
        return jax.shard_map(
            paired if short else per_device,
            mesh=mesh,
            in_specs=placed,
            out_specs=(P("ctx", "head"), P("ctx", "head"), P("ctx", "head"), P("ctx", "head")),
            check_vma=False,
        )(queries, keys, values, grad_out, log_decay, doc_lengths)

    return whole
```

```python
import jax
import jax.numpy as jnp
import functools

from jax import lax
from jax.experimental import pallas as pl
from jax.experimental.pallas import tpu as pltpu
from jax.sharding import PartitionSpec as P

BLOCK = 128


def passed_along(block, axis, distance):
    devices = range(lax.axis_size(axis))
    route = [(i - distance, i) for i in devices if i - distance in devices]
    return lax.ppermute(block, axis, route)


def document_ids(doc_lengths, first_place, span_length):
    starts = jnp.cumsum(doc_lengths, dtype=jnp.int32) - doc_lengths
    places = first_place - 1 + jnp.arange(span_length + 1, dtype=jnp.int32)
    return jnp.sum((starts[None, :] <= places[:, None]).astype(jnp.int32), axis=1) - 1


def decay_tables(log_rates, doc_ids, block_size, score_scaling):
    block_count = log_rates.shape[0] // block_size
    cumulated = jnp.cumsum(log_rates.reshape(block_count, block_size), axis=1)
    before = doc_ids[0 : block_count * block_size : block_size]
    own_ids = doc_ids[1:].reshape(block_count, block_size)
    carried = (own_ids == before[:, None]).astype(jnp.float32)
    last_ids = own_ids[:, block_size - 1]
    tail_mask = (own_ids == last_ids[:, None]).astype(jnp.float32)
    block_decay = jnp.exp(cumulated[:, block_size - 1]) * carried[:, block_size - 1]
    row_index = lax.broadcasted_iota(jnp.int32, (block_size, block_size), 0)
    column_index = lax.broadcasted_iota(jnp.int32, (block_size, block_size), 1)
    inside = (own_ids[:, :, None] == own_ids[:, None, :]) & (row_index >= column_index)[None]
    decay_gaps = cumulated[:, :, None] - cumulated[:, None, :]
    weights = jnp.where(inside, jnp.exp(jnp.where(inside, decay_gaps, 0.0)), 0.0) * score_scaling
    per_head_decay_rate = jnp.exp(cumulated) * carried
    tail_decay = jnp.exp(cumulated[:, block_size - 1 :] - cumulated) * tail_mask
    return (weights, per_head_decay_rate, tail_decay, block_decay)


def chain_combine(earlier, follower):
    return (earlier[0] * follower[0], follower[0] * earlier[1] + follower[1])


def offset_list(shard_total):
    return [1] + [1 << level for level in range((shard_total - 1).bit_length())]


def per_device(queries, keys, values, grad_out, log_decay, doc_lengths):
    query_rows, key_rows, value_rows = (
        lax.all_to_all(queries, "head", split_axis=1, concat_axis=0, tiled=True),
        lax.all_to_all(keys, "head", split_axis=1, concat_axis=0, tiled=True),
        lax.all_to_all(values, "head", split_axis=1, concat_axis=0, tiled=True),
    )
    tok_dev, key_dim = key_rows.shape
    value_dim = value_rows.shape[1]
    block_count = tok_dev // BLOCK
    score_scaling = (key_dim * BLOCK) ** (-0.5)
    shard_total = lax.axis_size("ctx")
    doc_ids = document_ids(doc_lengths, lax.axis_index("ctx") * tok_dev, tok_dev)
    weights, per_head_decay_rate, tail_decay, block_decay = decay_tables(
        log_decay[0], doc_ids, BLOCK, score_scaling
    )
    query_block_list = query_rows.reshape(block_count, BLOCK, key_dim)
    key_blocks = key_rows.reshape(block_count, BLOCK, key_dim)
    value_block_list = value_rows.reshape(block_count, BLOCK, value_dim)
    gradient_block_list = grad_out.reshape(block_count, BLOCK, value_dim)
    zero_state = jnp.zeros((key_dim, value_dim), jnp.float32)
    keyed_blocks = (key_blocks * tail_decay[:, :, None]).astype(jnp.bfloat16)
    updates = jnp.einsum(
        "ncd,nce->nde", keyed_blocks, value_block_list, preferred_element_type=jnp.float32
    )
    local_starts = []
    running = zero_state
    factor = jnp.float32(1.0)
    block_index = 0
    local_starts.append(running)
    carry_gains = factor
    running = block_decay[block_index] * running + updates[block_index]
    factor = factor * block_decay[block_index]
    shard_decay = factor
    current = (shard_decay, running)
    for position, offset in enumerate(offset_list(shard_total)):
        pulled = passed_along((current[0], current[1]), "ctx", offset)
        current = pulled if position == 0 else chain_combine(pulled, current)
    incoming = current[1]
    states = jnp.stack([carry_gains * incoming])
    queried = (query_block_list * (per_head_decay_rate * score_scaling)[:, :, None]).astype(
        jnp.bfloat16
    )
    back_updates = jnp.einsum(
        "ncd,nce->nde", queried, gradient_block_list, preferred_element_type=jnp.float32
    )
    local_ends = [zero_state] * block_count
    back_gains = [jnp.float32(1.0)] * block_count
    running = zero_state
    factor = jnp.float32(1.0)
    for block_index in reversed(range(block_count)):
        local_ends[block_index] = running
        back_gains[block_index] = factor
        running = block_decay[block_index] * running + back_updates[block_index]
        factor = factor * block_decay[block_index]
    current = (shard_decay, running)
    for position, offset in enumerate(offset_list(shard_total)):
        pulled = passed_along((current[0], current[1]), "ctx", -offset)
        current = pulled if position == 0 else chain_combine(pulled, current)
    arriving = current[1]
    ends = jnp.stack([back_gains[0] * arriving])
    lowered_state = states.astype(jnp.bfloat16)
    back_low = ends.astype(jnp.bfloat16)
    scores = jnp.einsum(
        "nid,njd->nij", query_block_list, key_blocks, preferred_element_type=jnp.float32
    )
    attention_weights = (scores * weights).astype(jnp.bfloat16)
    retained = (
        jnp.einsum(
            "xho,xoy->xhy", query_block_list, lowered_state, preferred_element_type=jnp.float32
        )
        * (per_head_decay_rate * score_scaling)[:, :, None]
    )
    retained = retained + jnp.einsum(
        "bcv,bvd->bcd", attention_weights, value_block_list, preferred_element_type=jnp.float32
    )
    score_gradient = jnp.einsum(
        "ysb,ytb->yst", gradient_block_list, value_block_list, preferred_element_type=jnp.float32
    )
    gprobs = (score_gradient * weights).astype(jnp.bfloat16)
    query_gradient = (
        jnp.einsum(
            "srj,sqj->srq", gradient_block_list, lowered_state, preferred_element_type=jnp.float32
        )
        * (per_head_decay_rate * score_scaling)[:, :, None]
    )
    query_gradient = query_gradient + jnp.einsum(
        "nij,njd->nid", gprobs, key_blocks, preferred_element_type=jnp.float32
    )
    grad_k = (
        jnp.einsum("nje,nde->njd", value_block_list, back_low, preferred_element_type=jnp.float32)
        * tail_decay[:, :, None]
    )
    grad_k = grad_k + jnp.einsum(
        "nij,nid->njd", gprobs, query_block_list, preferred_element_type=jnp.float32
    )
    value_gradient = (
        jnp.einsum("njd,nde->nje", key_blocks, back_low, preferred_element_type=jnp.float32)
        * tail_decay[:, :, None]
    )
    value_gradient = value_gradient + jnp.einsum(
        "glu,glx->gux", attention_weights, gradient_block_list, preferred_element_type=jnp.float32
    )
    return (
        retained.reshape(tok_dev, value_dim).astype(jnp.bfloat16),
        query_gradient.reshape(tok_dev, key_dim).astype(jnp.bfloat16),
        grad_k.reshape(tok_dev, key_dim).astype(jnp.bfloat16),
        value_gradient.reshape(tok_dev, value_dim).astype(jnp.bfloat16),
    )


CHUNKS = 4
PARTS = 2
MESH = pl.DeviceIdType.MESH
F32, BF16 = jnp.float32, jnp.bfloat16


def dot(left, right, left_dim, right_dim):
    return lax.dot_general(
        left, right, (((left_dim,), (right_dim,)), ((), ())), preferred_element_type=F32
    )


def kernel(
    shards,
    heads,
    q_ref, k_ref, v_ref, g_ref, log_hbm, len_hbm,
    ret_ref, dq_ref, dk_ref, dv_ref,
    q_all, k_all, v_all, g_all, log_ref, len_ref,
    u_buf, w_buf,
    f_first_out, f_first_in, f_state_out, f_state_in,
    b_first_out, b_first_in, b_state_out, b_state_in,
    ret_part, dq_part, dk_part, dv_part,
    head_send, head_recv, local_sem,
    f_first_send, f_first_recv, f_state_send, f_state_recv,
    b_first_send, b_first_recv, b_state_send, b_state_recv,
):
    c, h = lax.axis_index("ctx"), lax.axis_index("head")
    rows = q_ref.shape[0]
    tokens, key_dim = q_all.shape
    value_dim = v_all.shape[1]
    width = value_dim // CHUNKS
    part = value_dim // PARTS
    scale = (key_dim * BLOCK) ** -0.5
    even = lax.rem(c, 2) == 0
    odd = jnp.logical_not(even)
    has_earlier, has_later = c > 0, c < shards - 1

    def columns(n):
        return slice(n * width, (n + 1) * width)

    barrier = pltpu.get_barrier_semaphore()
    for offset in range(1, heads):
        pl.semaphore_signal(
            barrier, inc=1, device_id=(c, lax.rem(h + offset, heads)), device_id_type=MESH
        )

    @pl.when(has_earlier)
    def _():
        pl.semaphore_signal(barrier, inc=1, device_id=(c - 1, h), device_id_type=MESH)

    @pl.when(has_later)
    def _():
        pl.semaphore_signal(barrier, inc=1, device_id=(c + 1, h), device_id_type=MESH)

    def head_copy(number, target_head, place_head):
        if number < 2:
            source, gathered = ((q_ref, q_all), (k_ref, k_all))[number]
            span, place = key_dim, pl.ds(0, key_dim)
            begin = target_head * key_dim
        else:
            source, gathered, span = v_ref, v_all, part
            place = pl.ds((number - 2) * part, part)
            begin = target_head * value_dim + (number - 2) * part
        held = pl.ds(pl.multiple_of(place_head * rows, rows), rows)
        return source.at[:, pl.ds(pl.multiple_of(begin, span), span)], gathered.at[held, place]

    pieces = 2 + PARTS
    own = [
        pltpu.make_async_copy(*head_copy(number, h, h), local_sem.at[number])
        for number in range(pieces)
    ]
    small = [
        pltpu.make_async_copy(log_hbm, log_ref, local_sem.at[pieces]),
        pltpu.make_async_copy(len_hbm, len_ref, local_sem.at[pieces + 1]),
    ]
    own_g = pltpu.make_async_copy(g_ref, g_all, local_sem.at[pieces + 2])
    for copy in small + own[:1] + [own_g] + own[1:]:
        copy.start()

    pl.semaphore_wait(
        barrier, heads - 1 + has_earlier.astype(jnp.int32) + has_later.astype(jnp.int32)
    )

    def exchanged(number, offset, incoming):
        peer = lax.rem(h + (heads - offset if incoming else offset), heads)
        source, target = head_copy(number, peer, peer if incoming else h)
        return pltpu.make_async_remote_copy(
            src_ref=source, dst_ref=target,
            send_sem=head_send.at[number, offset - 1], recv_sem=head_recv.at[number, offset - 1],
            device_id=(c, peer), device_id_type=MESH,
        )

    for number in range(pieces):
        for offset in range(1, heads):
            exchanged(number, offset, False).start()

    def arrived(number):
        own[number].wait()
        for offset in range(1, heads):
            exchanged(number, offset, True).wait_recv()

    for copy in small:
        copy.wait()
    i = lax.broadcasted_iota(jnp.int32, (tokens, tokens), 0)
    j = lax.broadcasted_iota(jnp.int32, (tokens, tokens), 1)
    cum_col = jnp.sum(jnp.where(j <= i, log_ref[...], 0.0), axis=1, keepdims=True)
    cum_row = jnp.sum(jnp.where(i == j, cum_col, 0.0), axis=0, keepdims=True)
    documents = len_ref.shape[1]
    d = lax.broadcasted_iota(jnp.int32, (documents, documents), 0)
    e = lax.broadcasted_iota(jnp.int32, (documents, documents), 1)
    lengths = len_ref[...].astype(F32)
    starts = jnp.sum(jnp.where(e < d, lengths, 0.0), axis=1, keepdims=True)
    first = c * tokens
    places = (lax.broadcasted_iota(jnp.int32, (documents, tokens), 1) + first).astype(F32)
    doc_row = jnp.sum(jnp.where(starts <= places, 1.0, 0.0), axis=0, keepdims=True)
    before_place = (lax.broadcasted_iota(jnp.int32, (documents, 1), 1) + (first - 1)).astype(F32)
    doc_before = jnp.sum(jnp.where(starts <= before_place, 1.0, 0.0), axis=0, keepdims=True)
    doc_col = jnp.sum(jnp.where(i == j, doc_row, 0.0), axis=1, keepdims=True)
    last_lane = lax.broadcasted_iota(jnp.int32, (1, tokens), 1) == tokens - 1
    doc_last = jnp.sum(jnp.where(last_lane, doc_row, 0.0), axis=1, keepdims=True)
    cum_last = jnp.sum(jnp.where(last_lane, cum_row, 0.0), axis=1, keepdims=True)
    inside = (doc_col == doc_row) & (j <= i)
    weights = jnp.where(inside, jnp.exp(jnp.where(inside, cum_col - cum_row, 0.0)), 0.0) * scale
    rate = jnp.where(doc_col == doc_before, jnp.exp(cum_col), 0.0) * scale
    tail = jnp.where(doc_col == doc_last, jnp.exp(cum_last - cum_col), 0.0)
    decay = jnp.where(doc_last == doc_before, jnp.exp(cum_last), 0.0)

    def passing(update, first_out, first_in, state_out, state_in,
                first_send, first_recv, state_send, state_recv, opens, target, has_source, has_target):
        closes = jnp.logical_not(opens)

        def first_copy(n):
            return pltpu.make_async_remote_copy(
                src_ref=first_out.at[n], dst_ref=first_in.at[n],
                send_sem=first_send.at[n], recv_sem=first_recv.at[n],
                device_id=(target, h), device_id_type=MESH,
            )

        def state_copy(n):
            return pltpu.make_async_remote_copy(
                src_ref=state_out.at[n], dst_ref=state_in.at[n],
                send_sem=state_send.at[n], recv_sem=state_recv.at[n],
                device_id=(target, h), device_id_type=MESH,
            )

        def open_pair(n):
            @pl.when(opens)
            def _():
                first_out[n] = update[n].astype(BF16)
                first_copy(n).start()

        def close_pair():
            @pl.when(closes)
            def _():
                for n in range(CHUNKS):
                    close_chunk(n)

        def close_chunk(n):
            first_copy(n).wait_recv()

            @pl.when(has_target)
            def _():
                state_out[n] = (update[n] + decay * first_in[n].astype(F32)).astype(BF16)
                state_copy(n).start()

        def relay(n):
            @pl.when(has_source)
            def _():
                state_copy(n).wait_recv()

            @pl.when(jnp.logical_not(has_source))
            def _():
                state_in[n] = jnp.zeros(state_in.shape[1:], BF16)

            @pl.when(opens)
            def _():
                state_out[n] = (update[n] + decay * state_in[n].astype(F32)).astype(BF16)
                state_copy(n).start()

        def finish():
            @pl.when(opens)
            def _():
                for n in range(CHUNKS):
                    first_copy(n).wait_send()

            @pl.when(has_target)
            def _():
                for n in range(CHUNKS):
                    state_copy(n).wait_send()

        return open_pair, close_pair, close_chunk, relay, finish

    f_open, _, f_close_chunk, f_relay, f_finish = passing(
        u_buf, f_first_out, f_first_in, f_state_out, f_state_in,
        f_first_send, f_first_recv, f_state_send, f_state_recv,
        even, c + 1, has_earlier, has_later,
    )
    b_open, b_close, _, b_relay, b_finish = passing(
        w_buf, b_first_out, b_first_in, b_state_out, b_state_in,
        b_first_send, b_first_recv, b_state_send, b_state_recv,
        odd, c - 1, has_later, has_earlier,
    )

    per_part = CHUNKS // PARTS

    def halves(n):
        return slice(n * part, (n + 1) * part)

    own_g.wait()
    arrived(0)
    queried = (q_all[...].astype(F32) * rate).T.astype(BF16)
    for m in range(PARTS):
        product = dot(queried, g_all[:, halves(m)], 1, 0)
        for n in range(per_part):
            w_buf[m * per_part + n] = product[:, columns(n)]
            b_open(m * per_part + n)
    b_close()

    arrived(1)
    keyed = (k_all[...].astype(F32) * tail).T.astype(BF16)
    probs = (dot(q_all[...], k_all[...], 1, 1) * weights).astype(BF16)
    dv_part[...] = dot(probs, g_all[...], 0, 0)
    for m in range(PARTS):
        arrived(2 + m)
        product = dot(keyed, v_all[:, halves(m)], 1, 0)
        for n in range(per_part):
            u_buf[m * per_part + n] = product[:, columns(n)]
            f_open(m * per_part + n)

        @pl.when(odd)
        def _():
            for n in range(per_part):
                f_close_chunk(m * per_part + n)

    gprobs = (dot(g_all[...], v_all[...], 1, 1) * weights).astype(BF16)
    dk_part[...] = dot(gprobs, q_all[...], 0, 0)
    dq_part[...] = dot(gprobs, k_all[...], 1, 0)
    ret_part[...] = dot(probs, v_all[...], 1, 0)

    def directed(relay, state_in, left, right, factor, wide_part, narrow_part, wide_ref, narrow_ref, ahead):
        if ahead:
            for n in range(CHUNKS):
                relay(n)
        total = jnp.zeros((tokens, key_dim), F32)
        for m in range(PARTS):
            chunks = range(m * per_part, (m + 1) * per_part)
            if not ahead:
                for n in chunks:
                    relay(n)
            state = jnp.concatenate([state_in[n] for n in chunks], axis=1)
            wide_ref[:, halves(m)] = (
                dot(left[...], state, 1, 0) * factor + wide_part[:, halves(m)]
            ).astype(BF16)
            total += dot(right[:, halves(m)], state, 1, 1)
        narrow_ref[...] = (total * factor + narrow_part[...]).astype(BF16)

    forward = functools.partial(
        directed, f_relay, f_state_in, q_all, g_all, rate, ret_part, dq_part, ret_ref, dq_ref
    )
    backward = functools.partial(
        directed, b_relay, b_state_in, k_all, v_all, tail, dv_part, dk_part, dv_ref, dk_ref
    )

    backward(True)
    pl.when(even)(lambda: forward(True))
    pl.when(odd)(lambda: forward(False))

    for number in range(pieces):
        for offset in range(1, heads):
            exchanged(number, offset, False).wait_send()
    b_finish()
    f_finish()


def leave(*refs):
    count = len(refs) // 2
    sem = refs[-1]
    copies = [
        pltpu.make_async_copy(refs[n], refs[count + n], sem.at[n]) for n in range(count)
    ]
    for copy in copies:
        copy.start()
    for copy in copies:
        copy.wait()


def paired(queries, keys, values, grad_out, log_decay, doc_lengths):
    shards, heads = lax.axis_size("ctx"), lax.axis_size("head")
    tokens = queries.shape[0] * heads
    key_dim, value_dim = keys.shape[1] // heads, values.shape[1] // heads
    state = pltpu.VMEM((CHUNKS, key_dim, value_dim // CHUNKS), BF16)
    total = pltpu.VMEM((CHUNKS, key_dim, value_dim // CHUNKS), F32)
    dma = pltpu.SemaphoreType.DMA
    hbm, vmem = pl.BlockSpec(memory_space=pltpu.HBM), pl.BlockSpec(memory_space=pltpu.VMEM)
    wides = (value_dim, key_dim, key_dim, value_dim)
    outs = [jax.ShapeDtypeStruct((tokens, width), BF16) for width in wides]
    lengths = doc_lengths.reshape(1, -1)
    results = pl.pallas_call(
        functools.partial(kernel, shards, heads),
        out_shape=[pltpu.VMEM((tokens, width), BF16) for width in wides],
        in_specs=[hbm] * 6,
        out_specs=[vmem] * 4,
        scratch_shapes=[
            pltpu.VMEM((tokens, width), BF16) for width in (key_dim, key_dim, value_dim, value_dim)
        ]
        + [pltpu.VMEM(log_decay.shape, F32), pltpu.VMEM(lengths.shape, jnp.int32)]
        + [total] * 2
        + [state] * 8
        + [pltpu.VMEM((tokens, width), F32) for width in wides]
        + [dma((2 + PARTS, heads - 1)), dma((2 + PARTS, heads - 1)), dma((5 + PARTS,))]
        + [dma((CHUNKS,))] * 8,
        compiler_params=pltpu.CompilerParams(
            collective_id=0, has_side_effects=True, vmem_limit_bytes=40 * 1024 * 1024
        ),
    )(*[
        pltpu.with_memory_space_constraint(x, pltpu.HBM)
        for x in (queries, keys, values, grad_out, log_decay, lengths)
    ])
    return tuple(pl.pallas_call(
        leave,
        out_shape=outs,
        in_specs=[vmem] * 4,
        out_specs=[hbm] * 4,
        scratch_shapes=[dma((4,))],
        compiler_params=pltpu.CompilerParams(vmem_limit_bytes=1024 * 1024),
    )(*results))


def solution(mesh):
    shards, heads = mesh.shape["ctx"], mesh.shape["head"]

    def whole(queries, keys, values, grad_out, log_decay, doc_lengths):
        window = queries.shape[0]
        tokens = window // shards
        reach = -(-(window // 4 - 1) // tokens)
        short = reach <= 2 and shards % 2 == 0 and tokens == BLOCK and (tokens // heads) % 16 == 0
        placed = (
            P(("ctx", "head"), None),
            P(("ctx", "head"), None),
            P(("ctx", "head"), None),
            P("ctx", "head"),
            P("head", "ctx"),
            P(),
        )
        return jax.shard_map(
            paired if short else per_device,
            mesh=mesh,
            in_specs=placed,
            out_specs=(P("ctx", "head"), P("ctx", "head"), P("ctx", "head"), P("ctx", "head")),
            check_vma=False,
        )(queries, keys, values, grad_out, log_decay, doc_lengths)

    return whole
```

```python
import jax
import jax.numpy as jnp
import functools

from jax import lax
from jax.experimental import pallas as pl
from jax.experimental.pallas import tpu as pltpu
from jax.sharding import PartitionSpec as P

BLOCK = 128


def passed_along(block, axis, distance):
    devices = range(lax.axis_size(axis))
    route = [(i - distance, i) for i in devices if i - distance in devices]
    return lax.ppermute(block, axis, route)


def document_ids(doc_lengths, first_place, span_length):
    starts = jnp.cumsum(doc_lengths, dtype=jnp.int32) - doc_lengths
    places = first_place - 1 + jnp.arange(span_length + 1, dtype=jnp.int32)
    return jnp.sum((starts[None, :] <= places[:, None]).astype(jnp.int32), axis=1) - 1


def decay_tables(log_rates, doc_ids, block_size, score_scaling):
    block_count = log_rates.shape[0] // block_size
    cumulated = jnp.cumsum(log_rates.reshape(block_count, block_size), axis=1)
    before = doc_ids[0 : block_count * block_size : block_size]
    own_ids = doc_ids[1:].reshape(block_count, block_size)
    carried = (own_ids == before[:, None]).astype(jnp.float32)
    last_ids = own_ids[:, block_size - 1]
    tail_mask = (own_ids == last_ids[:, None]).astype(jnp.float32)
    block_decay = jnp.exp(cumulated[:, block_size - 1]) * carried[:, block_size - 1]
    row_index = lax.broadcasted_iota(jnp.int32, (block_size, block_size), 0)
    column_index = lax.broadcasted_iota(jnp.int32, (block_size, block_size), 1)
    inside = (own_ids[:, :, None] == own_ids[:, None, :]) & (row_index >= column_index)[None]
    decay_gaps = cumulated[:, :, None] - cumulated[:, None, :]
    weights = jnp.where(inside, jnp.exp(jnp.where(inside, decay_gaps, 0.0)), 0.0) * score_scaling
    per_head_decay_rate = jnp.exp(cumulated) * carried
    tail_decay = jnp.exp(cumulated[:, block_size - 1 :] - cumulated) * tail_mask
    return (weights, per_head_decay_rate, tail_decay, block_decay)


def chain_combine(earlier, follower):
    return (earlier[0] * follower[0], follower[0] * earlier[1] + follower[1])


def offset_list(shard_total):
    return [1] + [1 << level for level in range((shard_total - 1).bit_length())]


def per_device(queries, keys, values, grad_out, log_decay, doc_lengths):
    query_rows, key_rows, value_rows = (
        lax.all_to_all(queries, "head", split_axis=1, concat_axis=0, tiled=True),
        lax.all_to_all(keys, "head", split_axis=1, concat_axis=0, tiled=True),
        lax.all_to_all(values, "head", split_axis=1, concat_axis=0, tiled=True),
    )
    tok_dev, key_dim = key_rows.shape
    value_dim = value_rows.shape[1]
    block_count = tok_dev // BLOCK
    score_scaling = (key_dim * BLOCK) ** (-0.5)
    shard_total = lax.axis_size("ctx")
    doc_ids = document_ids(doc_lengths, lax.axis_index("ctx") * tok_dev, tok_dev)
    weights, per_head_decay_rate, tail_decay, block_decay = decay_tables(
        log_decay[0], doc_ids, BLOCK, score_scaling
    )
    query_block_list = query_rows.reshape(block_count, BLOCK, key_dim)
    key_blocks = key_rows.reshape(block_count, BLOCK, key_dim)
    value_block_list = value_rows.reshape(block_count, BLOCK, value_dim)
    gradient_block_list = grad_out.reshape(block_count, BLOCK, value_dim)
    zero_state = jnp.zeros((key_dim, value_dim), jnp.float32)
    keyed_blocks = (key_blocks * tail_decay[:, :, None]).astype(jnp.bfloat16)
    updates = jnp.einsum(
        "ncd,nce->nde", keyed_blocks, value_block_list, preferred_element_type=jnp.float32
    )
    local_starts = []
    running = zero_state
    factor = jnp.float32(1.0)
    block_index = 0
    local_starts.append(running)
    carry_gains = factor
    running = block_decay[block_index] * running + updates[block_index]
    factor = factor * block_decay[block_index]
    shard_decay = factor
    current = (shard_decay, running)
    for position, offset in enumerate(offset_list(shard_total)):
        pulled = passed_along((current[0], current[1]), "ctx", offset)
        current = pulled if position == 0 else chain_combine(pulled, current)
    incoming = current[1]
    states = jnp.stack([carry_gains * incoming])
    queried = (query_block_list * (per_head_decay_rate * score_scaling)[:, :, None]).astype(
        jnp.bfloat16
    )
    back_updates = jnp.einsum(
        "ncd,nce->nde", queried, gradient_block_list, preferred_element_type=jnp.float32
    )
    local_ends = [zero_state] * block_count
    back_gains = [jnp.float32(1.0)] * block_count
    running = zero_state
    factor = jnp.float32(1.0)
    for block_index in reversed(range(block_count)):
        local_ends[block_index] = running
        back_gains[block_index] = factor
        running = block_decay[block_index] * running + back_updates[block_index]
        factor = factor * block_decay[block_index]
    current = (shard_decay, running)
    for position, offset in enumerate(offset_list(shard_total)):
        pulled = passed_along((current[0], current[1]), "ctx", -offset)
        current = pulled if position == 0 else chain_combine(pulled, current)
    arriving = current[1]
    ends = jnp.stack([back_gains[0] * arriving])
    lowered_state = states.astype(jnp.bfloat16)
    back_low = ends.astype(jnp.bfloat16)
    scores = jnp.einsum(
        "nid,njd->nij", query_block_list, key_blocks, preferred_element_type=jnp.float32
    )
    attention_weights = (scores * weights).astype(jnp.bfloat16)
    retained = (
        jnp.einsum(
            "xho,xoy->xhy", query_block_list, lowered_state, preferred_element_type=jnp.float32
        )
        * (per_head_decay_rate * score_scaling)[:, :, None]
    )
    retained = retained + jnp.einsum(
        "bcv,bvd->bcd", attention_weights, value_block_list, preferred_element_type=jnp.float32
    )
    score_gradient = jnp.einsum(
        "ysb,ytb->yst", gradient_block_list, value_block_list, preferred_element_type=jnp.float32
    )
    gprobs = (score_gradient * weights).astype(jnp.bfloat16)
    query_gradient = (
        jnp.einsum(
            "srj,sqj->srq", gradient_block_list, lowered_state, preferred_element_type=jnp.float32
        )
        * (per_head_decay_rate * score_scaling)[:, :, None]
    )
    query_gradient = query_gradient + jnp.einsum(
        "nij,njd->nid", gprobs, key_blocks, preferred_element_type=jnp.float32
    )
    grad_k = (
        jnp.einsum("nje,nde->njd", value_block_list, back_low, preferred_element_type=jnp.float32)
        * tail_decay[:, :, None]
    )
    grad_k = grad_k + jnp.einsum(
        "nij,nid->njd", gprobs, query_block_list, preferred_element_type=jnp.float32
    )
    value_gradient = (
        jnp.einsum("njd,nde->nje", key_blocks, back_low, preferred_element_type=jnp.float32)
        * tail_decay[:, :, None]
    )
    value_gradient = value_gradient + jnp.einsum(
        "glu,glx->gux", attention_weights, gradient_block_list, preferred_element_type=jnp.float32
    )
    return (
        retained.reshape(tok_dev, value_dim).astype(jnp.bfloat16),
        query_gradient.reshape(tok_dev, key_dim).astype(jnp.bfloat16),
        grad_k.reshape(tok_dev, key_dim).astype(jnp.bfloat16),
        value_gradient.reshape(tok_dev, value_dim).astype(jnp.bfloat16),
    )


CHUNKS = 4
PARTS = 2
MESH = pl.DeviceIdType.MESH
F32, BF16 = jnp.float32, jnp.bfloat16


def dot(left, right, left_dim, right_dim):
    return lax.dot_general(
        left, right, (((left_dim,), (right_dim,)), ((), ())), preferred_element_type=F32
    )


def kernel(
    shards,
    heads,
    q_ref, k_ref, v_ref, g_ref, log_hbm, len_hbm,
    ret_ref, dq_ref, dk_ref, dv_ref,
    q_all, k_all, v_all, g_all, log_ref, len_ref,
    u_buf, w_buf,
    f_first_out, f_first_in, f_state_out, f_state_in,
    b_first_out, b_first_in, b_state_out, b_state_in,
    ret_part, dq_part, dk_part, dv_part,
    head_send, head_recv, local_sem,
    f_first_send, f_first_recv, f_state_send, f_state_recv,
    b_first_send, b_first_recv, b_state_send, b_state_recv,
):
    c, h = lax.axis_index("ctx"), lax.axis_index("head")
    rows = q_ref.shape[0]
    tokens, key_dim = q_all.shape
    value_dim = v_all.shape[1]
    width = value_dim // CHUNKS
    part = value_dim // PARTS
    scale = (key_dim * BLOCK) ** -0.5
    even = lax.rem(c, 2) == 0
    odd = jnp.logical_not(even)
    has_earlier, has_later = c > 0, c < shards - 1

    def columns(n):
        return slice(n * width, (n + 1) * width)

    barrier = pltpu.get_barrier_semaphore()
    for offset in range(1, heads):
        pl.semaphore_signal(
            barrier, inc=1, device_id=(c, lax.rem(h + offset, heads)), device_id_type=MESH
        )

    @pl.when(has_earlier)
    def _():
        pl.semaphore_signal(barrier, inc=1, device_id=(c - 1, h), device_id_type=MESH)

    @pl.when(has_later)
    def _():
        pl.semaphore_signal(barrier, inc=1, device_id=(c + 1, h), device_id_type=MESH)

    def head_copy(number, target_head, place_head):
        if number < 2:
            source, gathered = ((q_ref, q_all), (k_ref, k_all))[number]
            span, place = key_dim, pl.ds(0, key_dim)
            begin = target_head * key_dim
        else:
            source, gathered, span = v_ref, v_all, part
            place = pl.ds((number - 2) * part, part)
            begin = target_head * value_dim + (number - 2) * part
        held = pl.ds(pl.multiple_of(place_head * rows, rows), rows)
        return source.at[:, pl.ds(pl.multiple_of(begin, span), span)], gathered.at[held, place]

    pieces = 2 + PARTS
    own = [
        pltpu.make_async_copy(*head_copy(number, h, h), local_sem.at[number])
        for number in range(pieces)
    ]
    small = [
        pltpu.make_async_copy(log_hbm, log_ref, local_sem.at[pieces]),
        pltpu.make_async_copy(len_hbm, len_ref, local_sem.at[pieces + 1]),
    ]
    own_g = pltpu.make_async_copy(g_ref, g_all, local_sem.at[pieces + 2])
    for copy in small + own[:1] + [own_g] + own[1:]:
        copy.start()

    pl.semaphore_wait(
        barrier, heads - 1 + has_earlier.astype(jnp.int32) + has_later.astype(jnp.int32)
    )

    def exchanged(number, offset, incoming):
        peer = lax.rem(h + (heads - offset if incoming else offset), heads)
        source, target = head_copy(number, peer, peer if incoming else h)
        return pltpu.make_async_remote_copy(
            src_ref=source, dst_ref=target,
            send_sem=head_send.at[number, offset - 1], recv_sem=head_recv.at[number, offset - 1],
            device_id=(c, peer), device_id_type=MESH,
        )

    for number in range(pieces):
        for offset in range(1, heads):
            exchanged(number, offset, False).start()

    def arrived(number):
        own[number].wait()
        for offset in range(1, heads):
            exchanged(number, offset, True).wait_recv()

    for copy in small:
        copy.wait()
    i = lax.broadcasted_iota(jnp.int32, (tokens, tokens), 0)
    j = lax.broadcasted_iota(jnp.int32, (tokens, tokens), 1)
    cum_col = jnp.sum(jnp.where(j <= i, log_ref[...], 0.0), axis=1, keepdims=True)
    cum_row = jnp.sum(jnp.where(i == j, cum_col, 0.0), axis=0, keepdims=True)
    documents = len_ref.shape[1]
    d = lax.broadcasted_iota(jnp.int32, (documents, documents), 0)
    e = lax.broadcasted_iota(jnp.int32, (documents, documents), 1)
    lengths = len_ref[...].astype(F32)
    starts = jnp.sum(jnp.where(e < d, lengths, 0.0), axis=1, keepdims=True)
    first = c * tokens
    places = (lax.broadcasted_iota(jnp.int32, (documents, tokens), 1) + first).astype(F32)
    doc_row = jnp.sum(jnp.where(starts <= places, 1.0, 0.0), axis=0, keepdims=True)
    before_place = (lax.broadcasted_iota(jnp.int32, (documents, 1), 1) + (first - 1)).astype(F32)
    doc_before = jnp.sum(jnp.where(starts <= before_place, 1.0, 0.0), axis=0, keepdims=True)
    doc_col = jnp.sum(jnp.where(i == j, doc_row, 0.0), axis=1, keepdims=True)
    last_lane = lax.broadcasted_iota(jnp.int32, (1, tokens), 1) == tokens - 1
    doc_last = jnp.sum(jnp.where(last_lane, doc_row, 0.0), axis=1, keepdims=True)
    cum_last = jnp.sum(jnp.where(last_lane, cum_row, 0.0), axis=1, keepdims=True)
    inside = (doc_col == doc_row) & (j <= i)
    weights = jnp.where(inside, jnp.exp(jnp.where(inside, cum_col - cum_row, 0.0)), 0.0) * scale
    rate = jnp.where(doc_col == doc_before, jnp.exp(cum_col), 0.0) * scale
    tail = jnp.where(doc_col == doc_last, jnp.exp(cum_last - cum_col), 0.0)
    decay = jnp.where(doc_last == doc_before, jnp.exp(cum_last), 0.0)

    def passing(update, first_out, first_in, state_out, state_in,
                first_send, first_recv, state_send, state_recv, opens, target, has_source, has_target):
        closes = jnp.logical_not(opens)

        def first_copy(n):
            return pltpu.make_async_remote_copy(
                src_ref=first_out.at[n], dst_ref=first_in.at[n],
                send_sem=first_send.at[n], recv_sem=first_recv.at[n],
                device_id=(target, h), device_id_type=MESH,
            )

        def state_copy(n):
            return pltpu.make_async_remote_copy(
                src_ref=state_out.at[n], dst_ref=state_in.at[n],
                send_sem=state_send.at[n], recv_sem=state_recv.at[n],
                device_id=(target, h), device_id_type=MESH,
            )

        def open_pair(n):
            @pl.when(opens)
            def _():
                first_out[n] = update[n].astype(BF16)
                first_copy(n).start()

        def close_pair():
            @pl.when(closes)
            def _():
                for n in range(CHUNKS):
                    close_chunk(n)

        def close_chunk(n):
            first_copy(n).wait_recv()

            @pl.when(has_target)
            def _():
                state_out[n] = (update[n] + decay * first_in[n].astype(F32)).astype(BF16)
                state_copy(n).start()

        def relay(n):
            @pl.when(has_source)
            def _():
                state_copy(n).wait_recv()

            @pl.when(jnp.logical_not(has_source))
            def _():
                state_in[n] = jnp.zeros(state_in.shape[1:], BF16)

            @pl.when(opens)
            def _():
                state_out[n] = (update[n] + decay * state_in[n].astype(F32)).astype(BF16)
                state_copy(n).start()

        def finish():
            @pl.when(opens)
            def _():
                for n in range(CHUNKS):
                    first_copy(n).wait_send()

            @pl.when(has_target)
            def _():
                for n in range(CHUNKS):
                    state_copy(n).wait_send()

        return open_pair, close_pair, close_chunk, relay, finish

    f_open, _, f_close_chunk, f_relay, f_finish = passing(
        u_buf, f_first_out, f_first_in, f_state_out, f_state_in,
        f_first_send, f_first_recv, f_state_send, f_state_recv,
        even, c + 1, has_earlier, has_later,
    )
    b_open, b_close, _, b_relay, b_finish = passing(
        w_buf, b_first_out, b_first_in, b_state_out, b_state_in,
        b_first_send, b_first_recv, b_state_send, b_state_recv,
        odd, c - 1, has_later, has_earlier,
    )

    per_part = CHUNKS // PARTS

    def halves(n):
        return slice(n * part, (n + 1) * part)

    own_g.wait()
    arrived(0)
    queried = (q_all[...].astype(F32) * rate).T.astype(BF16)
    for m in range(PARTS):
        product = dot(queried, g_all[:, halves(m)], 1, 0)
        for n in range(per_part):
            w_buf[m * per_part + n] = product[:, columns(n)]
            b_open(m * per_part + n)
    b_close()

    arrived(1)
    keyed = (k_all[...].astype(F32) * tail).T.astype(BF16)
    probs = (dot(q_all[...], k_all[...], 1, 1) * weights).astype(BF16)
    dv_part[...] = dot(probs, g_all[...], 0, 0)
    for m in range(PARTS):
        arrived(2 + m)
        product = dot(keyed, v_all[:, halves(m)], 1, 0)
        for n in range(per_part):
            u_buf[m * per_part + n] = product[:, columns(n)]
            f_open(m * per_part + n)

        @pl.when(odd)
        def _():
            for n in range(per_part):
                f_close_chunk(m * per_part + n)

    @pl.when(odd)
    def _():
        for n in range(CHUNKS):
            b_relay(n)

    gprobs = (dot(g_all[...], v_all[...], 1, 1) * weights).astype(BF16)
    dk_part[...] = dot(gprobs, q_all[...], 0, 0)
    dq_part[...] = dot(gprobs, k_all[...], 1, 0)
    ret_part[...] = dot(probs, v_all[...], 1, 0)

    def directed(relay, state_in, left, right, factor, wide_part, narrow_part, wide_ref, narrow_ref, ahead):
        if ahead:
            for n in range(CHUNKS):
                relay(n)
        total = jnp.zeros((tokens, key_dim), F32)
        for m in range(PARTS):
            chunks = range(m * per_part, (m + 1) * per_part)
            if ahead is False:
                for n in chunks:
                    relay(n)
            state = jnp.concatenate([state_in[n] for n in chunks], axis=1)
            wide_ref[:, halves(m)] = (
                dot(left[...], state, 1, 0) * factor + wide_part[:, halves(m)]
            ).astype(BF16)
            total += dot(right[:, halves(m)], state, 1, 1)
        narrow_ref[...] = (total * factor + narrow_part[...]).astype(BF16)

    forward = functools.partial(
        directed, f_relay, f_state_in, q_all, g_all, rate, ret_part, dq_part, ret_ref, dq_ref
    )
    backward = functools.partial(
        directed, b_relay, b_state_in, k_all, v_all, tail, dv_part, dk_part, dv_ref, dk_ref
    )

    @pl.when(even)
    def _():
        backward(False)
        forward(True)

    @pl.when(odd)
    def _():
        backward(None)
        forward(False)

    for number in range(pieces):
        for offset in range(1, heads):
            exchanged(number, offset, False).wait_send()
    b_finish()
    f_finish()


def leave(*refs):
    count = len(refs) // 2
    sem = refs[-1]
    copies = [
        pltpu.make_async_copy(refs[n], refs[count + n], sem.at[n]) for n in range(count)
    ]
    for copy in copies:
        copy.start()
    for copy in copies:
        copy.wait()


def paired(queries, keys, values, grad_out, log_decay, doc_lengths):
    shards, heads = lax.axis_size("ctx"), lax.axis_size("head")
    tokens = queries.shape[0] * heads
    key_dim, value_dim = keys.shape[1] // heads, values.shape[1] // heads
    state = pltpu.VMEM((CHUNKS, key_dim, value_dim // CHUNKS), BF16)
    total = pltpu.VMEM((CHUNKS, key_dim, value_dim // CHUNKS), F32)
    dma = pltpu.SemaphoreType.DMA
    hbm, vmem = pl.BlockSpec(memory_space=pltpu.HBM), pl.BlockSpec(memory_space=pltpu.VMEM)
    wides = (value_dim, key_dim, key_dim, value_dim)
    outs = [jax.ShapeDtypeStruct((tokens, width), BF16) for width in wides]
    lengths = doc_lengths.reshape(1, -1)
    results = pl.pallas_call(
        functools.partial(kernel, shards, heads),
        out_shape=[pltpu.VMEM((tokens, width), BF16) for width in wides],
        in_specs=[hbm] * 6,
        out_specs=[vmem] * 4,
        scratch_shapes=[
            pltpu.VMEM((tokens, width), BF16) for width in (key_dim, key_dim, value_dim, value_dim)
        ]
        + [pltpu.VMEM(log_decay.shape, F32), pltpu.VMEM(lengths.shape, jnp.int32)]
        + [total] * 2
        + [state] * 8
        + [pltpu.VMEM((tokens, width), F32) for width in wides]
        + [dma((2 + PARTS, heads - 1)), dma((2 + PARTS, heads - 1)), dma((5 + PARTS,))]
        + [dma((CHUNKS,))] * 8,
        compiler_params=pltpu.CompilerParams(
            collective_id=0, has_side_effects=True, vmem_limit_bytes=40 * 1024 * 1024
        ),
    )(*[
        pltpu.with_memory_space_constraint(x, pltpu.HBM)
        for x in (queries, keys, values, grad_out, log_decay, lengths)
    ])
    return tuple(pl.pallas_call(
        leave,
        out_shape=outs,
        in_specs=[vmem] * 4,
        out_specs=[hbm] * 4,
        scratch_shapes=[dma((4,))],
        compiler_params=pltpu.CompilerParams(vmem_limit_bytes=1024 * 1024),
    )(*results))


def solution(mesh):
    shards, heads = mesh.shape["ctx"], mesh.shape["head"]

    def whole(queries, keys, values, grad_out, log_decay, doc_lengths):
        window = queries.shape[0]
        tokens = window // shards
        reach = -(-(window // 4 - 1) // tokens)
        short = reach <= 2 and shards % 2 == 0 and tokens == BLOCK and (tokens // heads) % 16 == 0
        placed = (
            P(("ctx", "head"), None),
            P(("ctx", "head"), None),
            P(("ctx", "head"), None),
            P("ctx", "head"),
            P("head", "ctx"),
            P(),
        )
        return jax.shard_map(
            paired if short else per_device,
            mesh=mesh,
            in_specs=placed,
            out_specs=(P("ctx", "head"), P("ctx", "head"), P("ctx", "head"), P("ctx", "head")),
            check_vma=False,
        )(queries, keys, values, grad_out, log_decay, doc_lengths)

    return whole
```
